32 devices in a mesh: groups: 2 (over y), seq: 4 (over z), dp: 4 (over x, core).
Axes of the slice: x: 2, y: 2, z: 4, core: 2. Of those that a mesh axis runs over, the one named last changes fastest.
Arguments:
- tokens: bfloat16 [8, 1536, 1024], P(('groups', 'dp'), 'seq'), parts along dimension 0, may hold values from -36 to 36
- segment_ids: int32 [8, 1536], P(('groups', 'dp'), 'seq'), parts along dimension 0, may hold values from 0 to 3, never falling along the last dimension, each value on 1 to 768 neighbouring positions
- norm_gain: float32 [1024], replicated, may hold values from 0.25 to 1.75
- w_qkv: bfloat16 [1024, 1536], P('dp'), may hold values from -0.1875 to 0.1875
- head_gain: float32 [512], replicated, may hold values from 0.25 to 1.75
- w_out: bfloat16 [512, 1024], P('dp'), may hold values from -0.25 to 0.25
- cotangent: bfloat16 [8, 1536, 1024], P(('groups', 'dp'), 'seq'), parts along dimension 0, may hold values from -6 to 6
Outputs:
- output: bfloat16 [8, 1536, 1024], P(('groups', 'dp'), 'seq'), parts along dimension 0
- grad_input: bfloat16 [8, 1536, 1024], P(('groups', 'dp'), 'seq'), parts along dimension 0
- grad_out_weight: float32 [1024, 1024], P(('groups', 'dp')), parts along dimension 0
The draws below stay inside these ranges and needn't reach their ends.
There are 2 independent parts, one for each index of `groups`. The reference program is written for one: setup_inputs(seed, part) draws one part's arguments, and reference() takes and returns one part's arrays. A program takes and returns all parts, laid end to end along the dimension named above; an argument that names none is the same for every part. Nothing has to cross between parts.
Inputs may be any that keep to these rules, and one draw needn't show every extreme that they name: `segment_ids`: within each micro-batch the segment numbers never fall along the samples, every number from 0 to 3 occurs, no segment has more than 768 samples, and one segment of each micro-batch has exactly 768.
All inputs are finite; a program needn't handle non-finite values.
Results may differ from the reference program's by a relative error of at most 0.0065.
Values may be sent and summed in bfloat16 or wider, within the bound.
No kernel may reach another device: no remote copies, remote signals or barrier semaphores. Data moves between devices by JAX's collectives and lax.ppermute only.
A program may use at most 128 MiB of HBM per device.

```python
import math
import jax
import jax.numpy as jnp
import numpy as np
from jax import lax

D = 1024
HEADS = 4
HEAD_DIM = 128
SEQ_DEV = 384
SEGS = 4
MB = 4
L = 1536
SEG_MOST = 768


def draw_tokens(key, part):
    base_key = jax.random.fold_in(key, 11)
    k_base, k_rows, k_cols = jax.random.split(base_key, 3)
    log_low = math.log(0.3)
    log_high = math.log(3.0)
    base = jnp.clip(jax.random.normal(k_base, (MB, L, D), jnp.float32), -4.0, 4.0)
    row_scale = jnp.exp(jax.random.uniform(k_rows, (MB, L, 1), jnp.float32, log_low, log_high))
    col_scale = jnp.exp(jax.random.uniform(k_cols, (1, 1, D), jnp.float32, log_low, log_high))
    return (base * row_scale * col_scale).astype(jnp.bfloat16)


def block_scale(stream_key, shape, cuts, least, largest):
    def one(dim, parts):
        steps = jax.random.uniform(jax.random.fold_in(jax.random.fold_in(stream_key, 6), dim), (parts,), jnp.float32, least / len(cuts), largest / len(cuts))
        return jnp.repeat(jnp.exp(steps), shape[dim] // parts).reshape((-1,) + (1,) * (len(shape) - dim - 1))

    level = one(*cuts[0])
    for cut in cuts[1:]:
        level = level * one(*cut)
    return level


def profile(count, total, reach, lean):
    loads = [(1 << 20) // math.isqrt(standing ** lean) + 1 for standing in range(2, count + 1)]
    rest, holding = total - reach - (count - 1), [1] * (count - 1)
    while rest > 0:
        candidates = [i for i in range(count - 1) if holding[i] < reach]
        pool, budget = sum([loads[i] for i in candidates]), rest
        for i in candidates:
            extra = min(reach - holding[i], max(1, budget * loads[i] // pool), rest)
            holding[i] = holding[i] + extra
            rest = rest - extra
    return np.array([reach] + holding)


def ragged(key, count, total, reach, slope):
    if count == 2:
        one = jax.random.randint(key, (), max(1, total - reach), min(reach, total - 1) + 1)
        return jnp.stack([one, total - one])
    tallies = jnp.asarray(profile(count, total, reach, slope), jnp.int32)
    pairs = (count - 1) // 2
    source_of, sink = tallies[1:1 + 2 * pairs:2], tallies[2:2 + 2 * pairs:2]
    margin = jnp.minimum(source_of - 1, reach - sink)
    shifted = jax.random.randint(jax.random.fold_in(key, 1), (pairs,), 0, 1 << 20) % (margin + 1)
    tallies = tallies.at[1:1 + 2 * pairs:2].set(source_of - shifted).at[2:2 + 2 * pairs:2].set(sink + shifted)
    return tallies[jax.random.permutation(jax.random.fold_in(key, 2), count)]


def noise(key, shape, spread, limit, shards=(), dtype=jnp.bfloat16):
    result = spread * jax.random.normal(key, shape, jnp.float32)
    if shards:
        result = result * block_scale(key, shape, shards, -0.22, 0.18)
    return jnp.clip(result, -limit, limit).astype(dtype)


def setup_inputs(seed: int = 0, part: int = 0) -> dict:
    key_of = jax.random.split(jax.random.key(seed), 8)
    own_keys = jax.random.split(jax.random.fold_in(key_of[7], part), 8)
    return {
        "tokens": draw_tokens(jax.random.fold_in(jax.random.fold_in(key_of[7], part), 71), part),
        "segment_ids": jax.vmap(lambda own: jnp.searchsorted(jnp.cumsum(ragged(own, SEGS, L, SEG_MOST, 2)), jnp.arange(L), side="right"))(jax.random.split(own_keys[1], MB)).reshape((MB, L)).astype(jnp.int32),
        "norm_gain": jnp.clip(1.0 + 0.15 * jax.random.normal(key_of[2], (D,), jnp.float32), 0.25, 1.75),
        "w_qkv": noise(key_of[3], (D, 3 * HEADS * HEAD_DIM), D ** -0.5, 0.1875, ((0, 4),)),
        "head_gain": jnp.clip(1.0 + 0.15 * jax.random.normal(key_of[4], (HEADS * HEAD_DIM,), jnp.float32), 0.25, 1.75),
        "w_out": noise(key_of[5], (HEADS * HEAD_DIM, D), (HEADS * HEAD_DIM) ** -0.5, 0.25, ((0, 4),)),
        "cotangent": noise(own_keys[6], (MB, L, D), 1.0, 6.0, ((0, 4), (1, 4))),
    }


epsilon = 1e-06

def feature_map(raw_value):
    return jnp.where(raw_value > 0, raw_value + 1.0, jnp.exp(jnp.minimum(raw_value, 0.0)))

def feature_slope(raw_value):
    return jnp.where(raw_value > 0, 1.0, jnp.exp(jnp.minimum(raw_value, 0.0)))

def to_blocks(array):
    reshaped = array.reshape((MB, L // SEQ_DEV, SEQ_DEV) + array.shape[2:])
    return jnp.moveaxis(reshaped, 1, 0)

def from_blocks(array):
    moved = jnp.moveaxis(array, 0, 1)
    return moved.reshape((MB, L) + array.shape[3:])

def block_mask(block_seg):
    same_seg = block_seg[:, :, None] == block_seg[:, None, :]
    causal_order = lax.broadcasted_iota(jnp.int32, (SEQ_DEV, SEQ_DEV), 0) >= lax.broadcasted_iota(jnp.int32, (SEQ_DEV, SEQ_DEV), 1)
    return (same_seg & causal_order[None]).astype(jnp.float32)

def widen(array):
    return array.astype(jnp.float32)

def reference(tokens, segment_ids, norm_gain, w_qkv, head_gain, w_out, cotangent):
    highest = lax.Precision.HIGHEST
    attn_width = HEADS * HEAD_DIM
    flat_in = tokens.reshape(-1, D).astype(jnp.float32)
    inv_rms = lax.rsqrt(lax.optimization_barrier(jnp.mean(flat_in * flat_in, axis=1, keepdims=True)) + epsilon)
    normed = (flat_in * inv_rms * norm_gain).astype(jnp.bfloat16)
    projected = jnp.dot(normed, w_qkv, preferred_element_type=jnp.float32).astype(jnp.bfloat16)
    shaped = projected.reshape(MB, L, 3, HEADS, HEAD_DIM)
    raw_q = shaped[:, :, 0]
    raw_k = shaped[:, :, 1]
    values = shaped[:, :, 2]
    feat_q = feature_map(widen(raw_q)).astype(jnp.bfloat16)
    feat_k = feature_map(widen(raw_k)).astype(jnp.bfloat16)
    seg_blocks = to_blocks(segment_ids)
    q_blocks = to_blocks(feat_q)
    k_blocks = to_blocks(feat_k)
    v_blocks = to_blocks(values)

    def forward_block(carry_pair, pieces):
        carry_id, carry_state = carry_pair
        block_q, block_k, block_v, block_seg = pieces
        causal = block_mask(block_seg)
        q_wide, k_wide, v_wide = (widen(block_q), widen(block_k), widen(block_v))
        scores = (jnp.einsum('mthd,mshd->mhts', q_wide, k_wide, precision=highest) * causal[:, None]).astype(jnp.bfloat16)
        intra_sum = jnp.einsum('mhts,mshe->mthe', widen(scores), v_wide, precision=highest)
        take_fwd = (block_seg == carry_id[:, None]).astype(jnp.float32)
        carried = jnp.einsum('mthd,mhde->mthe', q_wide, carry_state, precision=highest) * take_fwd[:, :, None, None]
        last_id = block_seg[:, -1]
        tail_mask = (block_seg == last_id[:, None]).astype(jnp.float32)
        block_state = jnp.einsum('mshd,mshe->mhde', k_wide * tail_mask[:, :, None, None], v_wide, precision=highest)
        keep_old = (carry_id == last_id).astype(jnp.float32)
        next_state = block_state + keep_old[:, None, None, None] * carry_state
        return ((last_id, next_state), (intra_sum + carried, carry_id, carry_state))
    start_pair = (jnp.full((MB,), -1, jnp.int32), jnp.zeros((MB, HEADS, HEAD_DIM, HEAD_DIM), jnp.float32))
    unused, (attn_blocks, fwd_ids, fwd_states) = lax.scan(forward_block, start_pair, (q_blocks, k_blocks, v_blocks, seg_blocks))
    attention = from_blocks(attn_blocks)
    norm_ratio = lax.rsqrt(lax.optimization_barrier(jnp.mean(attention * attention, axis=-1, keepdims=True)) + epsilon)
    head_scale = head_gain.reshape(HEADS, HEAD_DIM)
    mixed_out = (attention * norm_ratio * head_scale).astype(jnp.bfloat16).reshape(-1, attn_width)
    mapped = jnp.dot(mixed_out, w_out, preferred_element_type=jnp.float32)
    output = (flat_in + mapped).astype(jnp.bfloat16).reshape(MB, L, D)
    cot_flat = cotangent.reshape(-1, D)
    grad_out_weight = jnp.dot(mixed_out.T, cot_flat, preferred_element_type=jnp.float32) / math.sqrt(MB * L)
    d_mixed = jnp.dot(cot_flat, w_out.T, preferred_element_type=jnp.float32).reshape(MB, L, HEADS, HEAD_DIM)
    upstream = d_mixed * head_scale
    d_attn = (norm_ratio * upstream - norm_ratio ** 3 * attention * lax.optimization_barrier(jnp.mean(attention * upstream, axis=-1, keepdims=True))).astype(jnp.bfloat16)

    def backward_block(carry_pair, pieces):
        grad_id, grad_state = carry_pair
        block_q, block_k, block_v, block_seg, block_d, fwd_id, fwd_state = pieces
        causal = block_mask(block_seg)
        q_wide, k_wide, v_wide, d_wide = (widen(block_q), widen(block_k), widen(block_v), widen(block_d))
        scores = (jnp.einsum('mthd,mshd->mhts', q_wide, k_wide, precision=highest) * causal[:, None]).astype(jnp.bfloat16)
        d_scores = (jnp.einsum('mthe,mshe->mhts', d_wide, v_wide, precision=highest) * causal[:, None]).astype(jnp.bfloat16)
        take_fwd = (block_seg == fwd_id[:, None]).astype(jnp.float32)[:, :, None, None]
        take_back = (block_seg == grad_id[:, None]).astype(jnp.float32)[:, :, None, None]
        d_feat_q = jnp.einsum('mhts,mshd->mthd', widen(d_scores), k_wide, precision=highest) + jnp.einsum('mthe,mhde->mthd', d_wide, fwd_state, precision=highest) * take_fwd
        d_feat_k = jnp.einsum('mhts,mthd->mshd', widen(d_scores), q_wide, precision=highest) + jnp.einsum('mshe,mhde->mshd', v_wide, grad_state, precision=highest) * take_back
        d_values = jnp.einsum('mhts,mthe->mshe', widen(scores), d_wide, precision=highest) + jnp.einsum('mshd,mhde->mshe', k_wide, grad_state, precision=highest) * take_back
        first_id = block_seg[:, 0]
        head_mask = (block_seg == first_id[:, None]).astype(jnp.float32)
        block_grad = jnp.einsum('mthd,mthe->mhde', q_wide * head_mask[:, :, None, None], d_wide, precision=highest)
        keep_old = (grad_id == first_id).astype(jnp.float32)
        next_grad = block_grad + keep_old[:, None, None, None] * grad_state
        return ((first_id, next_grad), (d_feat_q, d_feat_k, d_values))
    unused_back, (dq_blocks, dk_blocks, dv_blocks) = lax.scan(backward_block, start_pair, (q_blocks, k_blocks, v_blocks, seg_blocks, to_blocks(d_attn), fwd_ids, fwd_states), reverse=True)
    d_q = (from_blocks(dq_blocks) * feature_slope(widen(raw_q))).astype(jnp.bfloat16)
    d_k = (from_blocks(dk_blocks) * feature_slope(widen(raw_k))).astype(jnp.bfloat16)
    d_v = from_blocks(dv_blocks).astype(jnp.bfloat16)
    d_proj = jnp.stack([d_q, d_k, d_v], axis=2).reshape(-1, 3 * attn_width)
    d_normed = jnp.dot(d_proj, w_qkv.T, preferred_element_type=jnp.float32)
    norm_grad = d_normed * norm_gain
    grad_flat = widen(cot_flat) + inv_rms * norm_grad - inv_rms ** 3 * flat_in * lax.optimization_barrier(jnp.mean(flat_in * norm_grad, axis=1, keepdims=True))
    grad_input = grad_flat.astype(jnp.bfloat16).reshape(MB, L, D)
    return (output, grad_input, grad_out_weight)
```

```python
import math

import jax
import jax.numpy as jnp
from jax import lax
from jax.experimental import pallas as pl
from jax.experimental.pallas import tpu as pltpu
from jax.sharding import PartitionSpec as P

D = 1024
HEADS = 4
HEAD_DIM = 128
ID_ROWS = 16
STATE_ROWS = HEADS * HEAD_DIM

epsilon = 1e-06

f32 = jnp.float32
bf16 = jnp.bfloat16


def dot_nn(a, b):
    return lax.dot_general(a, b, (((1,), (0,)), ((), ())), preferred_element_type=f32)


def dot_nt(a, b):
    return lax.dot_general(a, b, (((1,), (1,)), ((), ())), preferred_element_type=f32)


def dot_tn(a, b):
    return lax.dot_general(a, b, (((0,), (0,)), ((), ())), preferred_element_type=f32)


def feature_map(u):
    return jnp.where(u > 0, u + 1.0, jnp.exp(jnp.minimum(u, 0.0)))


def head(h):
    return slice(h * HEAD_DIM, (h + 1) * HEAD_DIM)


VMEM = pl.BlockSpec(memory_space=pltpu.VMEM)
SMEM = pl.BlockSpec(memory_space=pltpu.SMEM)


def call(body, outs, *args, scalars=0, scratch=()):
    return pl.pallas_call(
        body,
        scratch_shapes=[pltpu.VMEM(shape, dtype) for shape, dtype in scratch],
        out_shape=[jax.ShapeDtypeStruct(shape, dtype) for shape, dtype in outs],
        in_specs=[SMEM] * scalars + [VMEM] * (len(args) - scalars),
        out_specs=[VMEM] * len(outs),
        compiler_params=pltpu.CompilerParams(vmem_limit_bytes=40 * 1024 * 1024),
    )(*args)


def columns(index, width):
    return pl.ds(pl.multiple_of(index * width, width), width)


def prep_body(me, tokens, seg, gain, normed, inv_rms, mask, seg_col):
    x = tokens[...].astype(f32)
    inv = lax.rsqrt(jnp.mean(x * x, axis=1, keepdims=True) + epsilon)
    inv_rms[...] = inv
    for j in range(4):
        at = columns(me[0] ^ j, 256)
        normed[j] = (tokens[:, at].astype(f32) * inv * gain[:, at]).astype(bf16)
    length = seg.shape[1]
    across = jnp.broadcast_to(seg[...].astype(f32), (length, length))
    down = across.T
    order = lax.broadcasted_iota(jnp.int32, (length, length), 0) >= lax.broadcasted_iota(
        jnp.int32, (length, length), 1
    )
    mask[...] = jnp.where((across == down) & order, 1.0, 0.0)
    seg_col[...] = down[:, :HEAD_DIM]


def kv_body(normed, w0, w1, w2, w3, seg_col, feat_k, values, state):
    raw = dot_nn(normed[0], w0[...])
    raw += dot_nn(normed[1], w1[...])
    raw += dot_nn(normed[2], w2[...])
    raw += dot_nn(normed[3], w3[...])
    raw = raw.astype(bf16)
    length = normed.shape[1]
    last = seg_col[length - 1 : length, :]
    tail = seg_col[...] == last
    for h in range(HEADS):
        k = feature_map(raw[:, head(h)].astype(f32))
        v = raw[:, head(HEADS + h)]
        feat_k[h] = k.astype(bf16)
        values[h] = v
        state[head(h), :] = dot_tn(jnp.where(tail, k, 0.0).astype(bf16), v).astype(bf16)
    state[STATE_ROWS:, :] = jnp.broadcast_to(last, (ID_ROWS, HEAD_DIM)).astype(bf16)


def q_body(normed, w0, w1, w2, w3, feat_k, values, mask, feat_q, scores, intra):
    raw = dot_nn(normed[0], w0[...])
    raw += dot_nn(normed[1], w1[...])
    raw += dot_nn(normed[2], w2[...])
    raw += dot_nn(normed[3], w3[...])
    raw = raw.astype(bf16)
    for h in range(HEADS):
        q = feature_map(raw[:, head(h)].astype(f32)).astype(bf16)
        feat_q[h] = q
        s = (dot_nt(q, feat_k[h]) * mask[...]).astype(bf16)
        scores[h] = s
        intra[h] = dot_nn(s, values[h])


def mixed_grad_body(me, cot, o0, o1, o2, o3, gain, upstream):
    for j, o in enumerate((o0, o1, o2, o3)):
        h = me[0] ^ j
        upstream[h] = dot_nt(cot[...], o[...]) * gain[:, columns(h, HEAD_DIM)]


def joined(near, far, h):
    same = near[STATE_ROWS : STATE_ROWS + 1, :] == far[STATE_ROWS : STATE_ROWS + 1, :]
    total = near[head(h), :].astype(f32) + jnp.where(same, far[head(h), :].astype(f32), 0.0)
    return total.astype(bf16)


def attn_body(near, far, seg_col, feat_q, intra, upstream, gain, mixed, d_attn, state):
    first = seg_col[0:1, :]
    begin = seg_col[...] == first
    take = seg_col[...] == near[STATE_ROWS : STATE_ROWS + 1, :].astype(f32)
    for h in range(HEADS):
        q = feat_q[h]
        attention = intra[h] + jnp.where(take, dot_nn(q, joined(near, far, h)), 0.0)
        ratio = lax.rsqrt(jnp.mean(attention * attention, axis=1, keepdims=True) + epsilon)
        mixed[h] = (attention * ratio * gain[:, head(h)]).astype(bf16)
        up = upstream[h]
        inner = jnp.mean(attention * up, axis=1, keepdims=True)
        da = (ratio * up - ratio**3 * attention * inner).astype(bf16)
        d_attn[h] = da
        state[head(h), :] = dot_tn(jnp.where(begin, q.astype(f32), 0.0).astype(bf16), da).astype(bf16)
    state[STATE_ROWS:, :] = jnp.broadcast_to(first, (ID_ROWS, HEAD_DIM)).astype(bf16)


def weight_body(me, mixed, cot, keep, send):
    for j in range(4):
        part = dot_tn(mixed[me[0] ^ j], cot[...])
        if j % 2 == 0:
            keep[j // 2] = part
        else:
            send[j // 2] = part.astype(bf16)


def back_body(
    me, near, far, seg_col, mask, mixed, d_attn, values, feat_k, feat_q, scores,
    o0, o1, o2, o3, w0, w1, w2, w3, tokens, output, dk_intra, dv_intra, d_normed,
):
    take = seg_col[...] == near[STATE_ROWS : STATE_ROWS + 1, :].astype(f32)
    d_query = []
    for h in range(HEADS):
        da = d_attn[h]
        q = feat_q[h]
        ds = (dot_nt(da, values[h]) * mask[...]).astype(bf16)
        dq = dot_nn(ds, feat_k[h]) + jnp.where(take, dot_nt(da, joined(near, far, h)), 0.0)
        d_query.append((dq * jnp.minimum(q.astype(f32), 1.0)).astype(bf16))
        dk_intra[h] = dot_tn(ds, q)
        dv_intra[h] = dot_tn(scores[h], da)
    d_query = jnp.concatenate(d_query, axis=1)
    total = tokens[...].astype(f32)
    for j, (o, w) in enumerate(((o0, w0), (o1, w1), (o2, w2), (o3, w3))):
        total += dot_nn(mixed[me[0] ^ j], o[...])
        d_normed[j] = dot_nt(d_query, w[...])
    output[...] = total.astype(bf16)


def final_body(
    me, near, far, seg_col, feat_k, values, dk_intra, dv_intra, d_normed,
    w0, w1, w2, w3, tokens, cot, inv_rms, gain, grad, work,
):
    take = seg_col[...] == near[STATE_ROWS : STATE_ROWS + 1, :].astype(f32)
    d_key, d_value = [], []
    for h in range(HEADS):
        back = joined(near, far, h)
        k, v = feat_k[h], values[h]
        dk = dk_intra[h] + jnp.where(take, dot_nt(v, back), 0.0)
        dv = dv_intra[h] + jnp.where(take, dot_nn(k, back), 0.0)
        d_key.append((dk * jnp.minimum(k.astype(f32), 1.0)).astype(bf16))
        d_value.append(dv.astype(bf16))
    d_proj = jnp.concatenate(d_key + d_value, axis=1)
    inner = None
    for j, w in enumerate((w0, w1, w2, w3)):
        at = columns(me[0] ^ j, 256)
        norm_grad = (d_normed[j] + dot_nt(d_proj, w[...])) * gain[:, at]
        work[j] = norm_grad
        part = jnp.sum(tokens[:, at].astype(f32) * norm_grad, axis=1, keepdims=True)
        inner = part if inner is None else inner + part
    inv = inv_rms[...]
    scale = inv**3 * (inner * (1.0 / D))
    for j in range(4):
        at = columns(me[0] ^ j, 256)
        value = cot[:, at].astype(f32) + inv * work[j] - tokens[:, at].astype(f32) * scale
        grad[:, at] = value.astype(bf16)


def flip(array, axis, bit):
    n = lax.axis_size(axis)
    return lax.ppermute(array, axis, [(i, i ^ bit) for i in range(n)])


def shift(array, axis, step):
    n = lax.axis_size(axis)
    return lax.ppermute(array, axis, [(i, i + step) for i in range(n) if 0 <= i + step < n])


def carry(message, first, last, step):
    n = lax.axis_size("seq")
    if n <= 4:
        near = shift(message, "seq", step)
        return near, shift(near, "seq", step)
    position = lax.axis_index("seq")
    begin, end = (first, last) if step > 0 else (last, first)
    total = message[:STATE_ROWS].astype(f32)
    reach = 1
    while reach < n:
        before = shift(total, "seq", step * reach)
        ids = shift(jnp.stack([begin, end]), "seq", step * reach)
        there = position - step * reach
        there = (there >= 0) & (there < n)
        total = total + jnp.where(there & (begin == end) & (ids[1] == begin), before, 0.0)
        begin = jnp.where(there, ids[0], begin)
        reach *= 2
    rows = jnp.concatenate([total.astype(bf16), message[STATE_ROWS:]], axis=0)
    near = shift(rows, "seq", step)
    return near, jnp.zeros_like(near)


def gather(shard):
    other = flip(shard, "dp", 2)
    return [shard, flip(shard, "dp", 1), other, flip(other, "dp", 1)]


def reduce_weight(keep, send, scale):
    n = lax.axis_size("seq")
    odd = lax.axis_index("seq") % 2
    total = keep + flip(send, "dp", 1).astype(f32)
    rows = total.shape[1]
    half, quarter = rows // 2, rows // 4

    def part(array, start):
        return lax.dynamic_slice_in_dim(array, start, quarter, axis=-2)

    a_in = flip(total[1, :half].astype(bf16), "dp", 2)
    b_in = flip(part(total, half + (1 - odd) * quarter).astype(bf16), "seq", 1)
    a = total[0, :half] + a_in.astype(f32)
    b = part(total, half + odd * quarter) + b_in.astype(f32)
    b_next = flip(b[1].astype(bf16), "dp", 2)
    a_next = flip(part(a, (1 - odd) * quarter).astype(bf16), "seq", 1)
    mine = jnp.stack([part(a, odd * quarter) + a_next.astype(f32), b[0] + b_next.astype(f32)])
    reach = 2
    while reach < n:
        mine = mine + flip(mine.astype(bf16), "seq", reach).astype(f32)
        reach *= 2
    theirs = flip(mine.astype(bf16), "seq", 1).astype(f32)
    low = jnp.where(odd == 0, mine, theirs)
    high = jnp.where(odd == 0, theirs, mine)
    return jnp.stack([low, high], axis=1).reshape(rows, -1) * scale


def shards(tokens, segment_ids, norm_gain, w_qkv, head_gain, w_out, cotangent):
    length = segment_ids.shape[1]
    width = HEADS * HEAD_DIM
    me = lax.axis_index("dp").astype(jnp.int32).reshape(1)
    flat = tokens.reshape(length, D)
    cot = cotangent.reshape(length, D)
    gain = norm_gain.reshape(1, D)
    gain_h = head_gain.reshape(1, width)
    first = segment_ids[0, 0].astype(f32)
    last = segment_ids[0, -1].astype(f32)
    wide = (HEADS, length, HEAD_DIM)
    square = (HEADS, length, length)

    kv = gather(w_qkv[:, width:])
    wq = gather(w_qkv[:, :width])
    wo = gather(w_out)

    normed, inv_rms, mask, seg_col = call(
        prep_body,
        [((4, length, D // 4), bf16), ((length, 1), f32), ((length, length), f32), ((length, HEAD_DIM), f32)],
        me, flat, segment_ids, gain, scalars=1,
    )
    message = ((STATE_ROWS + ID_ROWS, HEAD_DIM), bf16)
    feat_k, values, state = call(
        kv_body, [(wide, bf16), (wide, bf16), message], normed, *kv, seg_col
    )
    near, far = carry(state, first, last, 1)
    feat_q, scores, intra = call(
        q_body, [(wide, bf16), (square, bf16), (wide, f32)], normed, *wq, feat_k, values, mask
    )
    (upstream,) = call(mixed_grad_body, [(wide, f32)], me, cot, *wo, gain_h, scalars=1)
    mixed, d_attn, back = call(
        attn_body,
        [(wide, bf16), (wide, bf16), message],
        near, far, seg_col, feat_q, intra, upstream, gain_h,
    )
    keep, send = call(
        weight_body,
        [((2, HEAD_DIM, D), f32), ((2, HEAD_DIM, D), bf16)],
        me, mixed, cot, scalars=1,
    )
    back_near, back_far = carry(back, first, last, -1)
    scale = 1.0 / math.sqrt(length * lax.axis_size("dp") * lax.axis_size("seq"))
    grad_out_weight = reduce_weight(keep, send, scale)
    output, dk_intra, dv_intra, d_normed = call(
        back_body,
        [((length, D), bf16), (wide, f32), (wide, f32), ((4, length, D // 4), f32)],
        me, near, far, seg_col, mask, mixed, d_attn, values, feat_k, feat_q, scores, *wo, *wq, flat, scalars=1,
    )
    (grad,) = call(
        final_body,
        [((length, D), bf16)],
        me, back_near, back_far, seg_col, feat_k, values, dk_intra, dv_intra, d_normed, *kv, flat, cot, inv_rms, gain,
        scalars=1, scratch=[((4, length, D // 4), f32)],
    )
    return (output.reshape(tokens.shape), grad.reshape(tokens.shape), grad_out_weight)


def solution(mesh):
    in_specs = (
        P(("groups", "dp"), "seq", None),
        P(("groups", "dp"), "seq"),
        P(),
        P("dp", None),
        P(),
        P("dp", None),
        P(("groups", "dp"), "seq", None),
    )
    out_specs = (
        P(("groups", "dp"), "seq", None),
        P(("groups", "dp"), "seq", None),
        P(("groups", "dp"), None),
    )
    return jax.shard_map(shards, mesh=mesh, in_specs=in_specs, out_specs=out_specs, check_vma=False)
```

```python
import math

import jax
import jax.numpy as jnp
from jax import lax
from jax.experimental import pallas as pl
from jax.experimental.pallas import tpu as pltpu
from jax.sharding import PartitionSpec as P

D = 1024
HEADS = 4
HEAD_DIM = 128
ID_ROWS = 16

epsilon = 1e-06

f32 = jnp.float32
bf16 = jnp.bfloat16


def dot_nn(a, b):
    return lax.dot_general(a, b, (((1,), (0,)), ((), ())), preferred_element_type=f32)


def dot_nt(a, b):
    return lax.dot_general(a, b, (((1,), (1,)), ((), ())), preferred_element_type=f32)


def dot_tn(a, b):
    return lax.dot_general(a, b, (((0,), (0,)), ((), ())), preferred_element_type=f32)


def feature_map(u):
    return jnp.where(u > 0, u + 1.0, jnp.exp(jnp.minimum(u, 0.0)))


def head(h):
    return slice(h * HEAD_DIM, (h + 1) * HEAD_DIM)


VMEM = pl.BlockSpec(memory_space=pltpu.VMEM)
SMEM = pl.BlockSpec(memory_space=pltpu.SMEM)


def call(body, outs, *args, scalars=0, scratch=()):
    return pl.pallas_call(
        body,
        scratch_shapes=[pltpu.VMEM(shape, dtype) for shape, dtype in scratch],
        out_shape=[jax.ShapeDtypeStruct(shape, dtype) for shape, dtype in outs],
        in_specs=[SMEM] * scalars + [VMEM] * (len(args) - scalars),
        out_specs=[VMEM] * len(outs),
        compiler_params=pltpu.CompilerParams(vmem_limit_bytes=16 * 1024 * 1024),
    )(*args)


def columns(index, width):
    return pl.ds(pl.multiple_of(index * width, width), width)


def prep_body(me, tokens, partner, seg, seg_partner, gain, normed, inv_rms, mask, seg_col):
    length = seg.shape[1]
    order = lax.broadcasted_iota(jnp.int32, (length, length), 0) >= lax.broadcasted_iota(
        jnp.int32, (length, length), 1
    )
    for i, (part, ids) in enumerate(((tokens, seg), (partner, seg_partner))):
        x = part[...].astype(f32)
        inv = lax.rsqrt(jnp.mean(x * x, axis=1, keepdims=True) + epsilon)
        if i == 0:
            inv_rms[...] = inv
        for j in range(4):
            at = columns(me[0] ^ j, 256)
            normed[j, i * length : (i + 1) * length] = (part[:, at].astype(f32) * inv * gain[:, at]).astype(bf16)
        across = jnp.broadcast_to(ids[...], (length, length))
        down = across.T
        mask[i] = jnp.where((across == down) & order, 1.0, 0.0)
        seg_col[i] = down[:, :HEAD_DIM]


def kv_near_body(normed, w0, w1, raw):
    raw[...] = dot_nn(normed[0], w0[...]) + dot_nn(normed[1], w1[...])


def kv_body(near, normed, w2, w3, seg_col, feat_k, values, state):
    raw = near[...] + dot_nn(normed[2], w2[...]) + dot_nn(normed[3], w3[...])
    raw = raw.astype(bf16)
    length = seg_col.shape[1]
    for i in range(2):
        last = seg_col[i, length - 1 : length, :]
        tail = seg_col[i] == last
        rows = slice(i * length, (i + 1) * length)
        for g in range(2):
            k = feature_map(raw[rows, head(g)].astype(f32))
            v = raw[rows, head(2 + g)]
            feat_k[i, g] = k.astype(bf16)
            values[i, g] = v
            state[i, head(g), :] = dot_tn(jnp.where(tail, k, 0.0).astype(bf16), v).astype(bf16)
        state[i, 2 * HEAD_DIM :, :] = jnp.broadcast_to(last, (ID_ROWS, HEAD_DIM)).astype(bf16)


def q_body(normed, w0, w1, w2, w3, feat_k, values, mask, feat_q, scores, intra):
    raw = dot_nn(normed[0], w0[...])
    raw += dot_nn(normed[1], w1[...])
    raw += dot_nn(normed[2], w2[...])
    raw += dot_nn(normed[3], w3[...])
    raw = raw.astype(bf16)
    length = mask.shape[1]
    for i in range(2):
        for g in range(2):
            q = feature_map(raw[i * length : (i + 1) * length, head(g)].astype(f32)).astype(bf16)
            feat_q[i, g] = q
            s = (dot_nt(q, feat_k[i, g]) * mask[i]).astype(bf16)
            scores[i, g] = s
            intra[i, g] = dot_nn(s, values[i, g])


def mixed_grad_body(me, cot, cot_partner, own, other, gain, upstream):
    for j, o in enumerate((own, other)):
        full = me[0] ^ (2 * j)
        for i, part in enumerate((cot, cot_partner)):
            upstream[i, full // 2] = dot_nt(part[...], o[...]) * gain[:, columns(full, HEAD_DIM)]


def id_of(message, i):
    return message[i, 2 * HEAD_DIM : 2 * HEAD_DIM + 1, :]


def joined(near, far, i, g):
    same = id_of(near, i) == id_of(far, i)
    total = near[i, head(g), :].astype(f32) + jnp.where(same, far[i, head(g), :].astype(f32), 0.0)
    return total.astype(bf16)


def attn_body(me, near, far, seg_col, feat_q, intra, upstream, gain, mixed, d_attn, state):
    for i in range(2):
        first = seg_col[i, 0:1, :]
        begin = seg_col[i] == first
        take = seg_col[i] == id_of(near, i).astype(f32)
        for g in range(2):
            q = feat_q[i, g]
            attention = intra[i, g] + jnp.where(take, dot_nn(q, joined(near, far, i, g)), 0.0)
            ratio = lax.rsqrt(jnp.mean(attention * attention, axis=1, keepdims=True) + epsilon)
            mixed[i, g] = (attention * ratio * gain[:, columns(2 * g + me[0] % 2, HEAD_DIM)]).astype(bf16)
            up = upstream[i, g]
            inner = jnp.mean(attention * up, axis=1, keepdims=True)
            da = (ratio * up - ratio**3 * attention * inner).astype(bf16)
            d_attn[i, g] = da
            state[i, head(g), :] = dot_tn(jnp.where(begin, q.astype(f32), 0.0).astype(bf16), da).astype(bf16)
        state[i, 2 * HEAD_DIM :, :] = jnp.broadcast_to(first, (ID_ROWS, HEAD_DIM)).astype(bf16)


def weight_body(me, odd, mixed, cot, cot_partner, a_keep, a_send, b_keep, b_send):
    half = HEAD_DIM // 2
    quarter = half // 2
    for j in range(2):
        g = (me[0] ^ (2 * j)) // 2
        part = dot_tn(mixed[0, g], cot[...]) + dot_tn(mixed[1, g], cot_partner[...])
        if j == 0:
            a_keep[...] = part[:half]
        else:
            a_send[...] = part[:half].astype(bf16)
        low, high = part[half : half + quarter], part[half + quarter :]
        second = odd[0] == 1
        b_keep[j] = jnp.where(second, high, low)
        b_send[j] = jnp.where(second, low, high).astype(bf16)


def back_body(
    me, near, far, seg_col, mask, mixed, d_attn, values, feat_k, feat_q, scores,
    own, other, w0, w1, w2, w3, tokens, out_own, out_partner, dk_intra, dv_intra, d_normed,
):
    length = mask.shape[1]
    for i in range(2):
        take = seg_col[i] == id_of(near, i).astype(f32)
        d_query = []
        for g in range(2):
            da = d_attn[i, g]
            q = feat_q[i, g]
            ds = (dot_nt(da, values[i, g]) * mask[i]).astype(bf16)
            dq = dot_nn(ds, feat_k[i, g]) + jnp.where(take, dot_nt(da, joined(near, far, i, g)), 0.0)
            d_query.append((dq * jnp.minimum(q.astype(f32), 1.0)).astype(bf16))
            dk_intra[i, g] = dot_tn(ds, q)
            dv_intra[i, g] = dot_tn(scores[i, g], da)
        d_query = jnp.concatenate(d_query, axis=1)
        for j, w in enumerate((w0, w1, w2, w3)):
            d_normed[j, i * length : (i + 1) * length] = dot_nt(d_query, w[...])
        total = dot_nn(mixed[i, me[0] // 2], own[...]) + dot_nn(mixed[i, 1 - me[0] // 2], other[...])
        if i == 0:
            out_own[...] = tokens[...].astype(f32) + total
        else:
            out_partner[...] = total.astype(bf16)


def key_value_body(
    near, far, seg_col, feat_k, values, dk_intra, dv_intra, d_normed, w0, w1, w2, w3, own, partner,
):
    length = seg_col.shape[1]
    for i in (1, 0):
        take = seg_col[i] == id_of(near, i).astype(f32)
        d_key, d_value = [], []
        for g in range(2):
            back = joined(near, far, i, g)
            k, v = feat_k[i, g], values[i, g]
            dk = dk_intra[i, g] + jnp.where(take, dot_nt(v, back), 0.0)
            dv = dv_intra[i, g] + jnp.where(take, dot_nn(k, back), 0.0)
            d_key.append((dk * jnp.minimum(k.astype(f32), 1.0)).astype(bf16))
            d_value.append(dv.astype(bf16))
        d_proj = jnp.concatenate(d_key + d_value, axis=1)
        for j, w in enumerate((w0, w1, w2, w3)):
            value = d_normed[j, i * length : (i + 1) * length] + dot_nt(d_proj, w[...])
            if i == 1:
                partner[j ^ 1] = value.astype(bf16)
            else:
                own[j] = value


def final_body(me, own, partner, tokens, cot, inv_rms, gain, grad, work):
    inner = None
    for j in range(4):
        at = columns(me[0] ^ j, 256)
        norm_grad = (own[j] + partner[j].astype(f32)) * gain[:, at]
        work[j] = norm_grad
        part = jnp.sum(tokens[:, at].astype(f32) * norm_grad, axis=1, keepdims=True)
        inner = part if inner is None else inner + part
    inv = inv_rms[...]
    scale = inv**3 * (inner * (1.0 / D))
    for j in range(4):
        at = columns(me[0] ^ j, 256)
        value = cot[:, at].astype(f32) + inv * work[j] - tokens[:, at].astype(f32) * scale
        grad[:, at] = value.astype(bf16)


def flip(array, axis, bit):
    n = lax.axis_size(axis)
    return lax.ppermute(array, axis, [(i, i ^ bit) for i in range(n)])


def shift(array, axis, step):
    n = lax.axis_size(axis)
    return lax.ppermute(array, axis, [(i, i + step) for i in range(n) if 0 <= i + step < n])


def carry(message, ends, step):
    n = lax.axis_size("seq")
    if n <= 4:
        near = shift(message, "seq", step)
        return near, shift(near, "seq", step)
    position = lax.axis_index("seq")
    begin, end = (ends[0], ends[1]) if step > 0 else (ends[1], ends[0])
    total = message[:, : 2 * HEAD_DIM].astype(f32)
    reach = 1
    while reach < n:
        before = shift(total, "seq", step * reach)
        ids = shift(jnp.stack([begin, end]), "seq", step * reach)
        there = position - step * reach
        there = (there >= 0) & (there < n)
        goes_on = there & (begin == end) & (ids[1] == begin)
        total = total + jnp.where(goes_on[:, None, None], before, 0.0)
        begin = jnp.where(there, ids[0], begin)
        reach *= 2
    rows = jnp.concatenate([total.astype(bf16), message[:, 2 * HEAD_DIM :]], axis=1)
    near = shift(rows, "seq", step)
    return near, jnp.zeros_like(near)


def reduce_weight(a_keep, a_send, b_keep, b_send, scale):
    n = lax.axis_size("seq")
    odd = lax.axis_index("seq") % 2
    rows = 2 * a_keep.shape[0]
    quarter = rows // 4
    a_in = flip(a_send, "dp", 2)
    b_in = flip(b_send, "seq", 1)
    a = a_keep + a_in.astype(f32)
    b = b_keep + b_in.astype(f32)
    low, high = a[:quarter], a[quarter:]
    a_next = flip(jnp.where(odd == 1, low, high).astype(bf16), "seq", 1)
    b_next = flip(b[1].astype(bf16), "dp", 2)
    mine = jnp.concatenate([jnp.where(odd == 1, high, low) + a_next.astype(f32), b[0] + b_next.astype(f32)])
    reach = 2
    while reach < n:
        mine = mine + flip(mine.astype(bf16), "seq", reach).astype(f32)
        reach *= 2
    theirs = flip(mine.astype(bf16), "seq", 1).astype(f32)
    low = jnp.where(odd == 0, mine, theirs)
    high = jnp.where(odd == 0, theirs, mine)
    return jnp.concatenate([low[:quarter], high[:quarter], low[quarter:], high[quarter:]]) * scale


def shards(tokens, segment_ids, norm_gain, w_qkv, head_gain, w_out, cotangent):
    length = segment_ids.shape[1]
    width = HEADS * HEAD_DIM
    dp = lax.axis_index("dp").astype(jnp.int32)
    me = dp.reshape(1)
    odd = (lax.axis_index("seq").astype(jnp.int32) % 2).reshape(1)
    flat = tokens.reshape(length, D)
    cot = cotangent.reshape(length, D)
    gain = norm_gain.reshape(1, D)
    gain_h = head_gain.reshape(1, width)
    seg = segment_ids.astype(f32)
    wide = (2, 2, length, HEAD_DIM)

    blocks = w_qkv.reshape(-1, 3, 2, 2, HEAD_DIM)

    def half(which):
        part = lax.dynamic_index_in_dim(blocks, which, axis=3, keepdims=False)
        rows = part.shape[0]
        return part[:, 0].reshape(rows, 2 * HEAD_DIM), part[:, 1:].reshape(rows, 4 * HEAD_DIM)

    q_mine, kv_mine = half(dp % 2)
    q_other, kv_other = half(1 - dp % 2)
    kv = [kv_mine, flip(kv_other, "dp", 1), flip(kv_mine, "dp", 2), flip(kv_other, "dp", 3)]
    partner = flip(flat, "dp", 1)
    seg_partner = flip(seg, "dp", 1)

    normed, inv_rms, mask, seg_col = call(
        prep_body,
        [
            ((4, 2 * length, D // 4), bf16),
            ((length, 1), f32),
            ((2, length, length), f32),
            ((2, length, HEAD_DIM), f32),
        ],
        me, flat, partner, seg, seg_partner, gain, scalars=1,
    )
    message = ((2, 2 * HEAD_DIM + ID_ROWS, HEAD_DIM), bf16)
    (raw_near,) = call(kv_near_body, [((2 * length, 4 * HEAD_DIM), f32)], normed, kv[0], kv[1])
    feat_k, values, state = call(
        kv_body, [(wide, bf16), (wide, bf16), message], raw_near, normed, kv[2], kv[3], seg_col
    )
    ends = jnp.stack([seg_col[:, 0, 0], seg_col[:, -1, 0]])
    near, far = carry(state, ends, 1)

    q_far, q_other, out_own, cot, state = lax.optimization_barrier((q_mine, q_other, w_out, cot, state))
    cot_partner = flip(cot, "dp", 1)
    wq = [q_mine, flip(q_other, "dp", 1), flip(q_far, "dp", 2), flip(q_other, "dp", 3)]
    out_other = flip(out_own, "dp", 2)
    feat_q, scores, intra = call(
        q_body,
        [(wide, bf16), ((2, 2, length, length), bf16), (wide, f32)],
        normed, *wq, feat_k, values, mask,
    )
    (upstream,) = call(
        mixed_grad_body, [(wide, f32)], me, cot, cot_partner, w_out, out_other, gain_h, scalars=1
    )
    mixed, d_attn, back = call(
        attn_body,
        [(wide, bf16), (wide, bf16), message],
        me, near, far, seg_col, feat_q, intra, upstream, gain_h, scalars=1,
    )
    rows = HEAD_DIM // 2
    parts = call(
        weight_body,
        [((rows, D), f32), ((rows, D), bf16), ((2, rows // 2, D), f32), ((2, rows // 2, D), bf16)],
        me, odd, mixed, cot, cot_partner, scalars=2,
    )
    back_near, back_far = carry(back, ends, -1)
    scale = 1.0 / math.sqrt(length * lax.axis_size("dp") * lax.axis_size("seq"))
    grad_out_weight = reduce_weight(*parts, scale)
    sums = (4, 2 * length, D // 4)
    out_sum, out_partner, dk_intra, dv_intra, d_normed = call(
        back_body,
        [((length, D), f32), ((length, D), bf16), (wide, f32), (wide, f32), (sums, f32)],
        me, near, far, seg_col, mask, mixed, d_attn, values, feat_k, feat_q, scores, w_out, out_other, *wq, flat,
        scalars=1,
    )
    output = (out_sum + flip(out_partner, "dp", 1).astype(f32)).astype(bf16)
    own, theirs = call(
        key_value_body,
        [((4, length, D // 4), f32), ((4, length, D // 4), bf16)],
        back_near, back_far, seg_col, feat_k, values, dk_intra, dv_intra, d_normed, *kv,
    )
    (grad,) = call(
        final_body,
        [((length, D), bf16)],
        me, own, flip(theirs, "dp", 1), flat, cot, inv_rms, gain,
        scalars=1, scratch=[((4, length, D // 4), f32)],
    )
    return (output.reshape(tokens.shape), grad.reshape(tokens.shape), grad_out_weight)


def solution(mesh):
    in_specs = (
        P(("groups", "dp"), "seq", None),
        P(("groups", "dp"), "seq"),
        P(),
        P("dp", None),
        P(),
        P("dp", None),
        P(("groups", "dp"), "seq", None),
    )
    out_specs = (
        P(("groups", "dp"), "seq", None),
        P(("groups", "dp"), "seq", None),
        P(("groups", "dp"), None),
    )
    return jax.shard_map(shards, mesh=mesh, in_specs=in_specs, out_specs=out_specs, check_vma=False)
```

```python
import functools
import math

import jax
import jax.numpy as jnp
from jax import lax
from jax.experimental import pallas as pl
from jax.experimental.pallas import tpu as pltpu
from jax.sharding import PartitionSpec as P

D = 1024
HEADS = 4
HEAD_DIM = 128
ID_ROWS = 16

epsilon = 1e-06

f32 = jnp.float32
bf16 = jnp.bfloat16


def dot_nn(a, b):
    return lax.dot_general(a, b, (((1,), (0,)), ((), ())), preferred_element_type=f32)


def dot_nt(a, b):
    return lax.dot_general(a, b, (((1,), (1,)), ((), ())), preferred_element_type=f32)


def dot_tn(a, b):
    return lax.dot_general(a, b, (((0,), (0,)), ((), ())), preferred_element_type=f32)


def feature_map(u):
    return jnp.where(u > 0, u + 1.0, jnp.exp(jnp.minimum(u, 0.0)))


def head(h):
    return slice(h * HEAD_DIM, (h + 1) * HEAD_DIM)


VMEM = pl.BlockSpec(memory_space=pltpu.VMEM)
SMEM = pl.BlockSpec(memory_space=pltpu.SMEM)
FAR = pl.BlockSpec(memory_space=pltpu.HBM)
FREE = pl.BlockSpec()


class Far:
    def __init__(self, array):
        self.array = array


class Fetched:
    def __init__(self, ref, copy):
        self.ref, self.copy = ref, copy

    def wait(self):
        if self.copy is not None:
            self.copy.wait()
            self.copy = None

    def __getitem__(self, index):
        self.wait()
        return self.ref[index]


def call(body, outs, scalars, *args, scratch=(), us=2.0):
    far = [isinstance(arg, Far) for arg in args]
    arrays = [arg.array if isinstance(arg, Far) else arg for arg in args]
    fetched = [arg for arg, is_far in zip(arrays, far) if is_far]

    def kernel(*refs):
        operands = refs[1 : 1 + len(arrays)]
        results = refs[1 + len(arrays) : 1 + len(arrays) + len(outs)]
        rest = refs[1 + len(arrays) + len(outs) :]
        given, at = [], 0
        for ref, is_far in zip(operands, far):
            if is_far:
                copy = pltpu.make_async_copy(ref, rest[at], rest[len(fetched)].at[at])
                copy.start()
                given.append(Fetched(rest[at], copy))
                at += 1
            else:
                given.append(ref)
        body(refs[0], *given, *results, *rest[len(fetched) + bool(fetched) :])
        for operand in given:
            if isinstance(operand, Fetched):
                operand.wait()

    buffers = [pltpu.VMEM(arg.shape, arg.dtype) for arg in fetched]
    if fetched:
        buffers.append(pltpu.SemaphoreType.DMA((len(fetched),)))
    return pl.pallas_call(
        kernel,
        out_shape=[jax.ShapeDtypeStruct(out[0], out[1]) for out in outs],
        in_specs=[SMEM] + [FAR if is_far else VMEM for is_far in far],
        out_specs=[out[2] if len(out) > 2 else VMEM for out in outs],
        scratch_shapes=buffers + [pltpu.VMEM(shape, dtype) for shape, dtype in scratch],
        compiler_params=pltpu.CompilerParams(vmem_limit_bytes=32 * 1024 * 1024),
        cost_estimate=pl.CostEstimate(flops=int(us * 1e9), transcendentals=0, bytes_accessed=int(us * 3e6)),
    )(scalars, *arrays)


def columns(index, width):
    return pl.ds(pl.multiple_of(index * width, width), width)


def causal(seg_col, seg_row, i):
    length = seg_row.shape[1]
    order = lax.broadcasted_iota(jnp.int32, (length, length), 0) >= lax.broadcasted_iota(
        jnp.int32, (length, length), 1
    )
    down = jnp.concatenate([seg_col[i]] * (length // HEAD_DIM), axis=1)
    return (down == seg_row[...]) & order


ME, ODD, NEAR, FURTHER, BACK_NEAR, BACK_FURTHER = range(6)


def split_body(info, w, kv_mine, kv_other, q_mine, q_other, sem):
    c = info[ME] % 2
    copies = []
    for kind, mine, other, first in ((4, kv_mine, kv_other, 0), (8, kv_mine, kv_other, 2), (0, q_mine, q_other, 0)):
        for target, which in ((mine, c), (other, 1 - c)):
            for g in range(2):
                copy = pltpu.make_async_copy(
                    w.at[:, columns(kind + 2 * g + which, HEAD_DIM)], target.at[:, head(first + g)], sem.at[len(copies)]
                )
                copy.start()
                copies.append(copy)
    for copy in copies:
        copy.wait()


def prep_body(info, tokens, partner, seg, seg_partner, gain, w0, w1, normed, inv_rms, seg_col, raw):
    length = seg.shape[1]
    for i, (part, ids) in enumerate(((tokens, seg), (partner, seg_partner))):
        x = part[...].astype(f32)
        inv = lax.rsqrt(jnp.mean(x * x, axis=1, keepdims=True) + epsilon)
        if i == 0:
            inv_rms[...] = inv
        for j in range(4):
            at = columns(info[ME] ^ j, 256)
            normed[j, i * length : (i + 1) * length] = (part[:, at].astype(f32) * inv * gain[:, at]).astype(bf16)
        seg_col[i] = jnp.broadcast_to(ids[...], (HEAD_DIM, length)).T
    raw[...] = dot_nn(normed[0], w0[...]) + dot_nn(normed[1], w1[...])


def kv_body(info, near, normed, w2, w3, seg_col, feat_k, values, state):
    raw = near[...] + dot_nn(normed[2], w2[...]) + dot_nn(normed[3], w3[...])
    raw = raw.astype(bf16)
    length = seg_col.shape[1]
    for i in range(2):
        last = seg_col[i, length - 1 : length, :]
        tail = seg_col[i] == last
        rows = slice(i * length, (i + 1) * length)
        for g in range(2):
            k = feature_map(raw[rows, head(g)].astype(f32))
            v = raw[rows, head(2 + g)]
            feat_k[i, g] = k.astype(bf16)
            values[i, g] = v
            state[i, head(g), :] = dot_tn(jnp.where(tail, k, 0.0).astype(bf16), v).astype(bf16)
        state[i, 2 * HEAD_DIM :, :] = jnp.broadcast_to(last, (ID_ROWS, HEAD_DIM)).astype(bf16)


def query_body(
    info, normed, w0, w1, w2, w3, feat_k, values, seg_col, seg, seg_partner, cot, cot_partner, own, other, gain,
    feat_q, intra, upstream,
):
    raw = dot_nn(normed[0], w0[...])
    raw += dot_nn(normed[1], w1[...])
    raw += dot_nn(normed[2], w2[...])
    raw += dot_nn(normed[3], w3[...])
    raw = raw.astype(bf16)
    length = seg.shape[1]
    for i, ids in enumerate((seg, seg_partner)):
        mask = causal(seg_col, ids, i)
        for g in range(2):
            q = feature_map(raw[i * length : (i + 1) * length, head(g)].astype(f32)).astype(bf16)
            feat_q[i, g] = q
            s = jnp.where(mask, dot_nt(q, feat_k[i, g]), 0.0).astype(bf16)
            intra[i, g] = dot_nn(s, values[i, g])
    for j, o in enumerate((own, other)):
        full = info[ME] ^ (2 * j)
        for i, part in enumerate((cot, cot_partner)):
            upstream[i, full // 2] = dot_nt(part[...], o[...]) * gain[:, columns(full, HEAD_DIM)]


def received(info, which, pair, middle, further, i):
    use_pair, use_further = info[which] == 1, info[which + 1] == 1
    near = jnp.where(use_pair, pair[i].astype(f32), middle[i].astype(f32))
    ids = near[2 * HEAD_DIM : 2 * HEAD_DIM + 1, :]
    far = further[i].astype(f32)
    same = (far[2 * HEAD_DIM : 2 * HEAD_DIM + 1, :] == ids) & use_further
    total = near[: 2 * HEAD_DIM] + jnp.where(same, far[: 2 * HEAD_DIM], 0.0)
    return ids, total.astype(bf16)


def attn_body(
    info, pair, middle, further, seg_col, feat_q, intra, upstream, gain, cot, cot_partner,
    mixed, d_attn, state, before, rest, a_send, b_send,
):
    for i in range(2):
        first = seg_col[i, 0:1, :]
        begin = seg_col[i] == first
        ids, total = received(info, NEAR, pair, middle, further, i)
        before[i] = total
        take = seg_col[i] == ids
        for g in range(2):
            q = feat_q[i, g]
            attention = intra[i, g] + jnp.where(take, dot_nn(q, total[head(g)]), 0.0)
            ratio = lax.rsqrt(jnp.mean(attention * attention, axis=1, keepdims=True) + epsilon)
            mixed[i, g] = (attention * ratio * gain[:, columns(2 * g + info[ME] % 2, HEAD_DIM)]).astype(bf16)
            up = upstream[i, g]
            inner = jnp.mean(attention * up, axis=1, keepdims=True)
            da = (ratio * up - ratio**3 * attention * inner).astype(bf16)
            d_attn[i, g] = da
            state[i, head(g), :] = dot_tn(jnp.where(begin, q.astype(f32), 0.0).astype(bf16), da).astype(bf16)
        state[i, 2 * HEAD_DIM :, :] = jnp.broadcast_to(first, (ID_ROWS, HEAD_DIM)).astype(bf16)
    half = HEAD_DIM // 2
    quarter = half // 2
    second = info[ODD] == 1
    for j in range(2):
        g = (info[ME] ^ (2 * j)) // 2
        part = dot_tn(mixed[0, g], cot[...]) + dot_tn(mixed[1, g], cot_partner[...])
        if j == 0:
            rest[:half] = part[:half]
        else:
            a_send[...] = part[:half].astype(bf16)
        low, high = part[half : half + quarter], part[half + quarter :]
        rest[half + j * quarter : half + (j + 1) * quarter] = jnp.where(second, high, low)
        b_send[j] = jnp.where(second, low, high).astype(bf16)


def weight_one_body(info, rest, a_in, b_in, kept, a_send, b_send):
    second = info[ODD] == 1
    quarter = b_in.shape[1]
    low = rest[:quarter] + a_in[:quarter].astype(f32)
    high = rest[quarter : 2 * quarter] + a_in[quarter:].astype(f32)
    kept[:quarter] = jnp.where(second, high, low)
    a_send[...] = jnp.where(second, low, high).astype(bf16)
    kept[quarter:] = rest[2 * quarter : 3 * quarter] + b_in[0].astype(f32)
    b_send[...] = (rest[3 * quarter :] + b_in[1].astype(f32)).astype(bf16)


def weight_two_body(info, kept, a_in, b_in, total, send):
    quarter = a_in.shape[0]
    total[:quarter] = kept[:quarter] + a_in[...].astype(f32)
    total[quarter:] = kept[quarter:] + b_in[...].astype(f32)
    send[...] = total[...].astype(bf16)


def weight_three_body(info, kept, arrived, total, send):
    total[...] = kept[...] + arrived[...].astype(f32)
    send[...] = total[...].astype(bf16)


def weight_last_body(scale, info, kept, arrived, grad):
    quarter = kept.shape[0] // 2
    second = info[ODD] == 1
    mine, theirs = kept[...] * scale, arrived[...].astype(f32) * scale
    low = jnp.where(second, theirs, mine)
    high = jnp.where(second, mine, theirs)
    for n, part in enumerate((low[:quarter], high[:quarter], low[quarter:], high[quarter:])):
        grad[n * quarter : (n + 1) * quarter] = part


def back_body(
    info, pair, before, middle, seg_col, seg, seg_partner, d_attn, values, feat_k, feat_q, mixed, own, other,
    d_query, dk_intra, dv_intra, out_partner,
):
    x = info[ME] // 2
    out_partner[...] = (dot_nn(mixed[1, x], own[...]) + dot_nn(mixed[1, 1 - x], other[...])).astype(bf16)
    for i, row in enumerate((seg, seg_partner)):
        mask = causal(seg_col, row, i)
        use_pair = info[NEAR] == 1
        last = 2 * HEAD_DIM
        ids = jnp.where(use_pair, pair[i, last : last + 1].astype(f32), middle[i, last : last + 1].astype(f32))
        take = seg_col[i] == ids
        for g in range(2):
            da, q, k = d_attn[i, g], feat_q[i, g], feat_k[i, g]
            s = jnp.where(mask, dot_nt(q, k), 0.0).astype(bf16)
            ds = jnp.where(mask, dot_nt(da, values[i, g]), 0.0).astype(bf16)
            dq = dot_nn(ds, k) + jnp.where(take, dot_nt(da, before[i, head(g)]), 0.0)
            d_query[i, :, head(g)] = (dq * jnp.minimum(q.astype(f32), 1.0)).astype(bf16)
            dk_intra[i, g] = dot_tn(ds, q)
            dv_intra[i, g] = dot_tn(s, da)


def output_body(info, tokens, partner, mixed, own, other, output):
    x = info[ME] // 2
    total = dot_nn(mixed[0, x], own[...]) + dot_nn(mixed[0, 1 - x], other[...])
    output[...] = (tokens[...].astype(f32) + (total + partner[...].astype(f32))).astype(bf16)


def project_back_body(
    info, pair, middle, further, seg_col, feat_k, values, dk_intra, dv_intra, d_query,
    q0, q1, q2, q3, w0, w1, w2, w3, own, partner,
):
    for i in (1, 0):
        ids, total = received(info, BACK_NEAR, pair, middle, further, i)
        take = seg_col[i] == ids
        d_key, d_value = [], []
        for g in range(2):
            back = total[head(g)]
            k, v = feat_k[i, g], values[i, g]
            dk = dk_intra[i, g] + jnp.where(take, dot_nt(v, back), 0.0)
            dv = dv_intra[i, g] + jnp.where(take, dot_nn(k, back), 0.0)
            d_key.append((dk * jnp.minimum(k.astype(f32), 1.0)).astype(bf16))
            d_value.append(dv.astype(bf16))
        d_proj = jnp.concatenate(d_key + d_value, axis=1)
        for j, (q, w) in enumerate(((q0, w0), (q1, w1), (q2, w2), (q3, w3))):
            value = dot_nt(d_query[i], q[...]) + dot_nt(d_proj, w[...])
            if i == 1:
                partner[j ^ 1] = value.astype(bf16)
            else:
                own[j] = value


def final_body(info, own, partner, tokens, cot, inv_rms, gain, grad, work):
    inner = None
    for j in range(4):
        at = columns(info[ME] ^ j, 256)
        norm_grad = (own[j] + partner[j].astype(f32)) * gain[:, at]
        work[j] = norm_grad
        part = jnp.sum(tokens[:, at].astype(f32) * norm_grad, axis=1, keepdims=True)
        inner = part if inner is None else inner + part
    inv = inv_rms[...]
    scale = inv**3 * (inner * (1.0 / D))
    for j in range(4):
        at = columns(info[ME] ^ j, 256)
        value = cot[:, at].astype(f32) + inv * work[j] - tokens[:, at].astype(f32) * scale
        grad[:, at] = value.astype(bf16)


def flip(array, axis, bit):
    n = lax.axis_size(axis)
    return lax.ppermute(array, axis, [(i, i ^ bit) for i in range(n)])


def shift(array, axis, step):
    n = lax.axis_size(axis)
    return lax.ppermute(array, axis, [(i, i + step) for i in range(n) if 0 <= i + step < n])


def carry(message, ends, step):
    n = lax.axis_size("seq")
    if n == 4:
        middle = lax.ppermute(message, "seq", [(1, 2), (2, 1)])
        return flip(message, "seq", 1), middle, flip(message, "seq", 2)
    position = lax.axis_index("seq")
    begin, end = (ends[0], ends[1]) if step > 0 else (ends[1], ends[0])
    total = message[:, : 2 * HEAD_DIM].astype(f32)
    reach = 1
    while reach < n:
        before = shift(total, "seq", step * reach)
        ids = shift(jnp.stack([begin, end]), "seq", step * reach)
        there = position - step * reach
        there = (there >= 0) & (there < n)
        goes_on = there & (begin == end) & (ids[1] == begin)
        total = total + jnp.where(goes_on[:, None, None], before, 0.0)
        begin = jnp.where(there, ids[0], begin)
        reach *= 2
    rows = jnp.concatenate([total.astype(bf16), message[:, 2 * HEAD_DIM :]], axis=1)
    near = shift(rows, "seq", step)
    return near, near, near


def reduce_weight(info, rest, a_send, b_send, scale):
    n = lax.axis_size("seq")
    half, width = a_send.shape
    quarter = half // 2
    kept, a_send, b_send = call(
        weight_one_body,
        [((half, width), f32), ((quarter, width), bf16), ((quarter, width), bf16)],
        info, rest, flip(a_send, "dp", 2), flip(b_send, "seq", 1),
    )
    outs = [((half, width), f32), ((half, width), bf16)]
    kept, send = call(weight_two_body, outs, info, kept, flip(a_send, "seq", 1), flip(b_send, "dp", 2))
    reach = 2
    while reach < n:
        kept, send = call(weight_three_body, outs, info, kept, flip(send, "seq", reach))
        reach *= 2
    (grad,) = call(
        functools.partial(weight_last_body, scale),
        [((2 * half, width), f32, FREE)],
        info, kept, flip(send, "seq", 1),
    )
    return grad


def shards(tokens, segment_ids, norm_gain, w_qkv, head_gain, w_out, cotangent):
    length = segment_ids.shape[1]
    width = HEADS * HEAD_DIM
    dp = lax.axis_index("dp").astype(jnp.int32)
    at = lax.axis_index("seq").astype(jnp.int32)
    n = lax.axis_size("seq")
    if n == 4:
        facts = [dp, at % 2, at % 2, at // 2, 1 - at % 2, 1 - at // 2]
    else:
        facts = [dp, at % 2, 0 * at, 0 * at, 0 * at, 0 * at]
    info = jnp.stack(facts)
    flat = tokens.reshape(length, D)
    cot = cotangent.reshape(length, D)
    gain = norm_gain.reshape(1, D)
    gain_h = head_gain.reshape(1, width)
    seg = segment_ids.astype(f32)
    wide = (2, 2, length, HEAD_DIM)
    shard_rows = w_qkv.shape[0]

    kv_mine, kv_other, q_mine, q_other = pl.pallas_call(
        split_body,
        out_shape=[jax.ShapeDtypeStruct((shard_rows, m * HEAD_DIM), bf16) for m in (4, 4, 2, 2)],
        in_specs=[SMEM, FAR],
        out_specs=[VMEM] * 4,
        scratch_shapes=[pltpu.SemaphoreType.DMA((12,))],
    )(info, w_qkv)
    kv = [kv_mine, flip(kv_other, "dp", 1), flip(kv_mine, "dp", 2), flip(kv_other, "dp", 3)]
    partner = flip(flat, "dp", 1)
    seg_partner = flip(seg, "dp", 1)

    normed, inv_rms, seg_col, raw_near = call(
        prep_body,
        [
            ((4, 2 * length, D // 4), bf16),
            ((length, 1), f32),
            ((2, length, HEAD_DIM), f32),
            ((2 * length, 4 * HEAD_DIM), f32),
        ],
        info, Far(flat), Far(partner), seg, seg_partner, gain, kv[0], kv[1], us=20.0,
    )
    kv[2], q_mine, q_other, out_own, cot = lax.optimization_barrier((kv[2], q_mine, q_other, w_out, cot))
    cot_partner = flip(cot, "dp", 1)
    wq = [q_mine, flip(q_other, "dp", 1), flip(q_mine, "dp", 2), flip(q_other, "dp", 3)]
    out_other = flip(out_own, "dp", 2)

    message = ((2, 2 * HEAD_DIM + ID_ROWS, HEAD_DIM), bf16)
    feat_k, values, state = call(
        kv_body, [(wide, bf16), (wide, bf16), message], info, raw_near, normed, kv[2], kv[3], seg_col
    )
    ends = jnp.stack([seg_col[:, 0, 0], seg_col[:, -1, 0]])
    near = carry(state, ends, 1)
    feat_q, intra, upstream = call(
        query_body,
        [(wide, bf16), (wide, f32), (wide, f32)],
        info, Far(normed), *map(Far, wq), feat_k, values, seg_col, seg, seg_partner,
        Far(cot), Far(cot_partner), Far(w_out), Far(out_other), gain_h,
    )
    rows = HEAD_DIM // 2
    mixed, d_attn, back, before, rest, a_send, b_send = call(
        attn_body,
        [
            (wide, bf16),
            (wide, bf16),
            message,
            ((2, 2 * HEAD_DIM, HEAD_DIM), bf16),
            ((2 * rows, D), f32),
            ((rows, D), bf16),
            ((2, rows // 2, D), bf16),
        ],
        info, *near, seg_col, feat_q, intra, upstream, gain_h, Far(cot), Far(cot_partner),
    )
    back_near = carry(back, ends, -1)
    scale = 1.0 / math.sqrt(length * lax.axis_size("dp") * n)
    grad_out_weight = reduce_weight(info, rest, a_send, b_send, scale)
    d_query, dk_intra, dv_intra, out_partner = call(
        back_body,
        [((2, length, 2 * HEAD_DIM), bf16), (wide, f32), (wide, f32), ((length, D), bf16)],
        info, near[0], before, near[1], seg_col, seg, seg_partner, d_attn, values, feat_k, feat_q, mixed,
        Far(w_out), Far(out_other),
    )
    (output,) = call(
        output_body,
        [((length, D), bf16, FREE)],
        info, Far(flat), Far(flip(out_partner, "dp", 1)), mixed, Far(w_out), Far(out_other),
    )
    own, theirs = call(
        project_back_body,
        [((4, length, D // 4), f32), ((4, length, D // 4), bf16)],
        info, *back_near, seg_col, feat_k, values, dk_intra, dv_intra, d_query, *map(Far, wq), *map(Far, kv),
    )
    (grad,) = call(
        final_body,
        [((length, D), bf16, FREE)],
        info, own, flip(theirs, "dp", 1), Far(flat), Far(cot), inv_rms, gain,
        scratch=[((4, length, D // 4), f32)],
    )
    return (output.reshape(tokens.shape), grad.reshape(tokens.shape), grad_out_weight)


def solution(mesh):
    in_specs = (
        P(("groups", "dp"), "seq", None),
        P(("groups", "dp"), "seq"),
        P(),
        P("dp", None),
        P(),
        P("dp", None),
        P(("groups", "dp"), "seq", None),
    )
    out_specs = (
        P(("groups", "dp"), "seq", None),
        P(("groups", "dp"), "seq", None),
        P(("groups", "dp"), None),
    )
    return jax.shard_map(shards, mesh=mesh, in_specs=in_specs, out_specs=out_specs, check_vma=False)
```

```python
import functools
import math

import jax
import jax.numpy as jnp
from jax import lax
from jax.experimental import pallas as pl
from jax.experimental.pallas import tpu as pltpu
from jax.sharding import PartitionSpec as P

D = 1024
HEADS = 4
HEAD_DIM = 128
ID_ROWS = 16

epsilon = 1e-06
W1, W2, W3 = 8.0, 8.0, 8.0

f32 = jnp.float32
bf16 = jnp.bfloat16


def dot_nn(a, b):
    return lax.dot_general(a, b, (((1,), (0,)), ((), ())), preferred_element_type=f32)


def dot_nt(a, b):
    return lax.dot_general(a, b, (((1,), (1,)), ((), ())), preferred_element_type=f32)


def dot_tn(a, b):
    return lax.dot_general(a, b, (((0,), (0,)), ((), ())), preferred_element_type=f32)


def feature_map(u):
    return jnp.where(u > 0, u + 1.0, jnp.exp(jnp.minimum(u, 0.0)))


def head(h):
    return slice(h * HEAD_DIM, (h + 1) * HEAD_DIM)


VMEM = pl.BlockSpec(memory_space=pltpu.VMEM)
ANY = pl.BlockSpec(memory_space=pl.ANY)


def call(body, outs, *args, scratch=(), us=2.0):
    return pl.pallas_call(
        body,
        out_shape=[jax.ShapeDtypeStruct(shape, dtype) for shape, dtype in outs],
        in_specs=[VMEM] * len(args),
        out_specs=[VMEM] * len(outs),
        scratch_shapes=[pltpu.VMEM(shape, dtype) for shape, dtype in scratch],
        compiler_params=pltpu.CompilerParams(vmem_limit_bytes=16 * 1024 * 1024),
        cost_estimate=pl.CostEstimate(flops=int(us * 1e9), transcendentals=0, bytes_accessed=int(us * 3e6)),
    )(*args)


def columns(index, width):
    return pl.ds(pl.multiple_of(index * width, width), width)


def causal(seg_col, seg_row, i):
    length = seg_row.shape[2]
    order = lax.broadcasted_iota(jnp.int32, (length, length), 0) >= lax.broadcasted_iota(
        jnp.int32, (length, length), 1
    )
    down = jnp.concatenate([seg_col[i]] * (length // HEAD_DIM), axis=1)
    return (down == seg_row[i]) & order


def split_body(w, kv_mine, kv_other, sem):
    c = lax.axis_index("dp") % 2
    copies = []
    for target, which in ((kv_mine, c), (kv_other, 1 - c)):
        for n in range(4):
            at = columns(4 + 4 * (n // 2) + 2 * (n % 2) + which, HEAD_DIM)
            copies.append(pltpu.make_async_copy(w.at[:, at], target.at[:, head(n)], sem.at[len(copies)]))
    for copy in copies:
        copy.start()
    for copy in copies:
        copy.wait()


def pack_body(w, w_out, seg, kv_other, pair, far, q_other, sem):
    c = lax.axis_index("dp") % 2
    rows, half = w_out.shape[0], w_out.shape[1] // 2
    full = w.shape[0]
    copies = [
        (w_out.at[:, :half], far.at[:rows, 2 * HEAD_DIM :]),
        (w_out.at[:, half:], far.at[rows:, 2 * HEAD_DIM :]),
    ]
    for g in range(2):
        mine, other = columns(2 * g + c, HEAD_DIM), columns(2 * g + 1 - c, HEAD_DIM)
        copies.append((w.at[:, mine], far.at[:, head(g)]))
        copies.append((w.at[:, other], q_other.at[:, head(g)]))
        copies.append((w.at[:, other], pair.at[:full, head(4 + g)]))
    copies = [pltpu.make_async_copy(source, target, sem.at[n]) for n, (source, target) in enumerate(copies)]
    for copy in copies:
        copy.start()
    pair[:full, KV_COLUMNS] = kv_other[...]
    pair[full:, : seg.shape[1]] = jnp.broadcast_to(seg[...].astype(f32), (ID_ROWS, seg.shape[1])).astype(bf16)
    for copy in copies:
        copy.wait()


def split(w):
    out = jax.ShapeDtypeStruct((w.shape[0], 4 * HEAD_DIM), bf16)
    return pl.pallas_call(
        split_body,
        out_shape=[out, out],
        in_specs=[ANY],
        out_specs=[VMEM, VMEM],
        scratch_shapes=[pltpu.SemaphoreType.DMA((8,))],
        cost_estimate=pl.CostEstimate(flops=10**9, transcendentals=0, bytes_accessed=10**6),
    )(w)


def pack(w, w_out, seg, kv_other):
    rows = w.shape[0]
    return pl.pallas_call(
        pack_body,
        out_shape=[
            jax.ShapeDtypeStruct((rows + ID_ROWS, 6 * HEAD_DIM), bf16),
            jax.ShapeDtypeStruct((rows, 6 * HEAD_DIM), bf16),
            jax.ShapeDtypeStruct((rows, 2 * HEAD_DIM), bf16),
        ],
        in_specs=[ANY, ANY, VMEM, VMEM],
        out_specs=[VMEM] * 3,
        scratch_shapes=[pltpu.SemaphoreType.DMA((8,))],
        cost_estimate=pl.CostEstimate(flops=10**9, transcendentals=0, bytes_accessed=10**6),
    )(w, w_out, seg, kv_other)


KV_COLUMNS = slice(0, 4 * HEAD_DIM)
PAIR_Q_COLUMNS = slice(4 * HEAD_DIM, 6 * HEAD_DIM)
FAR_Q_COLUMNS = slice(0, 2 * HEAD_DIM)


def out_rows(far):
    rows = far.shape[0] // 2
    return jnp.concatenate([far[:rows, 2 * HEAD_DIM :], far[rows:, 2 * HEAD_DIM :]], axis=1)


def pair_ids(pair, length):
    return pair[pair.shape[0] - ID_ROWS : pair.shape[0] - ID_ROWS + 1, :length].astype(f32)


def sources(step):
    at, n = lax.axis_index("seq"), lax.axis_size("seq")
    if n != 4:
        return at < 0, at < 0
    return (at % 2 == 1, at >= 2) if step > 0 else (at % 2 == 0, at < 2)


def prep_body(tokens, partner, seg, gain, w0, pair, normed, inv_rms, seg_col, seg_row, raw):
    length = seg.shape[1]
    for i, (part, ids) in enumerate(((tokens, seg[...].astype(f32)), (partner, pair_ids(pair, length)))):
        x = part[...].astype(f32)
        inv = lax.rsqrt(jnp.mean(x * x, axis=1, keepdims=True) + epsilon)
        if i == 0:
            inv_rms[...] = inv
        for j in range(4):
            at = columns(lax.axis_index("dp") ^ j, 256)
            normed[j, i * length : (i + 1) * length] = (part[:, at].astype(f32) * inv * gain[:, at]).astype(bf16)
        seg_row[i] = ids
        seg_col[i] = jnp.broadcast_to(ids, (HEAD_DIM, length)).T
    rows = w0.shape[0]
    raw[...] = dot_nn(normed[0], w0[...]) + dot_nn(normed[1], pair[:rows, KV_COLUMNS])


def kv_body(near, normed, w2, w3, seg_col, feat_k, values, state):
    raw = near[...] + dot_nn(normed[2], w2[...]) + dot_nn(normed[3], w3[...])
    raw = raw.astype(bf16)
    length = seg_col.shape[1]
    for i in range(2):
        last = seg_col[i, length - 1 : length, :]
        tail = seg_col[i] == last
        rows = slice(i * length, (i + 1) * length)
        for g in range(2):
            k = feature_map(raw[rows, head(g)].astype(f32))
            v = raw[rows, head(2 + g)]
            feat_k[i, g] = k.astype(bf16)
            values[i, g] = v
            state[i, head(g), :] = dot_tn(jnp.where(tail, k, 0.0).astype(bf16), v).astype(bf16)
        state[i, 2 * HEAD_DIM :, :] = jnp.broadcast_to(last, (ID_ROWS, HEAD_DIM)).astype(bf16)


def query_body(
    normed, own, pair, other, w3, feat_k, values, seg_col, seg_row, cot, cot_partner, gain,
    feat_q, intra, upstream,
):
    rows, length = own.shape[0], seg_row.shape[2]
    raw = dot_nn(normed[0], own[:, FAR_Q_COLUMNS])
    raw += dot_nn(normed[1], pair[:rows, PAIR_Q_COLUMNS])
    raw += dot_nn(normed[2], other[:, FAR_Q_COLUMNS])
    raw += dot_nn(normed[3], w3[...])
    raw = raw.astype(bf16)
    for i in range(2):
        mask = causal(seg_col, seg_row, i)
        for g in range(2):
            q = feature_map(raw[i * length : (i + 1) * length, head(g)].astype(f32)).astype(bf16)
            feat_q[i, g] = q
            s = jnp.where(mask, dot_nt(q, feat_k[i, g]), 0.0).astype(bf16)
            intra[i, g] = dot_nn(s, values[i, g])
    for j, o in enumerate((out_rows(own), out_rows(other))):
        full = lax.axis_index("dp") ^ (2 * j)
        for i, part in enumerate((cot, cot_partner)):
            upstream[i, full // 2] = dot_nt(part[...], o) * gain[:, columns(full, HEAD_DIM)]


def received(step, pair, middle, further, i):
    use_pair, use_further = sources(step)
    near = jnp.where(use_pair, pair[i].astype(f32), middle[i].astype(f32))
    ids = near[2 * HEAD_DIM : 2 * HEAD_DIM + 1, :]
    far = further[i].astype(f32)
    same = (far[2 * HEAD_DIM : 2 * HEAD_DIM + 1, :] == ids) & use_further
    total = near[: 2 * HEAD_DIM] + jnp.where(same, far[: 2 * HEAD_DIM], 0.0)
    return ids, total.astype(bf16)


def attn_body(
    pair, middle, further, seg_col, feat_q, intra, upstream, gain, cot, cot_partner,
    mixed, d_attn, state, before, rest, a_send, b_send,
):
    for i in range(2):
        first = seg_col[i, 0:1, :]
        begin = seg_col[i] == first
        ids, total = received(1, pair, middle, further, i)
        before[i] = total
        take = seg_col[i] == ids
        for g in range(2):
            q = feat_q[i, g]
            attention = intra[i, g] + jnp.where(take, dot_nn(q, total[head(g)]), 0.0)
            ratio = lax.rsqrt(jnp.mean(attention * attention, axis=1, keepdims=True) + epsilon)
            mixed[i, g] = (attention * ratio * gain[:, columns(2 * g + lax.axis_index("dp") % 2, HEAD_DIM)]).astype(bf16)
            up = upstream[i, g]
            inner = jnp.mean(attention * up, axis=1, keepdims=True)
            da = (ratio * up - ratio**3 * attention * inner).astype(bf16)
            d_attn[i, g] = da
            state[i, head(g), :] = dot_tn(jnp.where(begin, q.astype(f32), 0.0).astype(bf16), da).astype(bf16)
        state[i, 2 * HEAD_DIM :, :] = jnp.broadcast_to(first, (ID_ROWS, HEAD_DIM)).astype(bf16)
    half = HEAD_DIM // 2
    quarter = half // 2
    second = lax.axis_index("seq") % 2 == 1
    for j in range(2):
        g = (lax.axis_index("dp") ^ (2 * j)) // 2
        part = dot_tn(mixed[0, g], cot[...]) + dot_tn(mixed[1, g], cot_partner[...])
        if j == 0:
            rest[:half] = part[:half]
        else:
            a_send[...] = part[:half].astype(bf16)
        low, high = part[half : half + quarter], part[half + quarter :]
        rest[half + j * quarter : half + (j + 1) * quarter] = jnp.where(second, high, low)
        b_send[j] = jnp.where(second, low, high).astype(bf16)


def weight_one_body(rest, a_in, b_in, kept, a_send, b_send):
    second = lax.axis_index("seq") % 2 == 1
    quarter = b_in.shape[1]
    low = rest[:quarter] + a_in[:quarter].astype(f32)
    high = rest[quarter : 2 * quarter] + a_in[quarter:].astype(f32)
    kept[:quarter] = jnp.where(second, high, low)
    a_send[...] = jnp.where(second, low, high).astype(bf16)
    kept[quarter:] = rest[2 * quarter : 3 * quarter] + b_in[0].astype(f32)
    b_send[...] = (rest[3 * quarter :] + b_in[1].astype(f32)).astype(bf16)


def weight_two_body(kept, a_in, b_in, total, send):
    quarter = a_in.shape[0]
    total[:quarter] = kept[:quarter] + a_in[...].astype(f32)
    total[quarter:] = kept[quarter:] + b_in[...].astype(f32)
    send[...] = total[...].astype(bf16)


def weight_three_body(kept, arrived, total, send):
    total[...] = kept[...] + arrived[...].astype(f32)
    send[...] = total[...].astype(bf16)


def weight_last_body(scale, kept, arrived, grad):
    quarter = kept.shape[0] // 2
    second = lax.axis_index("seq") % 2 == 1
    mine, theirs = kept[...] * scale, arrived[...].astype(f32) * scale
    low = jnp.where(second, theirs, mine)
    high = jnp.where(second, mine, theirs)
    for n, part in enumerate((low[:quarter], high[:quarter], low[quarter:], high[quarter:])):
        grad[n * quarter : (n + 1) * quarter] = part


def back_body(
    pair, before, middle, seg_col, seg_row, d_attn, values, feat_k, feat_q, mixed, own, other,
    d_query, dk_intra, dv_intra, out_partner,
):
    x = lax.axis_index("dp") // 2
    out_partner[...] = (dot_nn(mixed[1, x], out_rows(own)) + dot_nn(mixed[1, 1 - x], out_rows(other))).astype(bf16)
    for i in range(2):
        mask = causal(seg_col, seg_row, i)
        use_pair, _ = sources(1)
        last = 2 * HEAD_DIM
        ids = jnp.where(use_pair, pair[i, last : last + 1].astype(f32), middle[i, last : last + 1].astype(f32))
        take = seg_col[i] == ids
        for g in range(2):
            da, q, k = d_attn[i, g], feat_q[i, g], feat_k[i, g]
            s = jnp.where(mask, dot_nt(q, k), 0.0).astype(bf16)
            ds = jnp.where(mask, dot_nt(da, values[i, g]), 0.0).astype(bf16)
            dq = dot_nn(ds, k) + jnp.where(take, dot_nt(da, before[i, head(g)]), 0.0)
            d_query[i, :, head(g)] = (dq * jnp.minimum(q.astype(f32), 1.0)).astype(bf16)
            dk_intra[i, g] = dot_tn(ds, q)
            dv_intra[i, g] = dot_tn(s, da)


def output_body(tokens, partner, mixed, own, other, output):
    x = lax.axis_index("dp") // 2
    total = dot_nn(mixed[0, x], out_rows(own)) + dot_nn(mixed[0, 1 - x], out_rows(other))
    output[...] = (tokens[...].astype(f32) + (total + partner[...].astype(f32))).astype(bf16)


def project_back_body(
    pair, middle, further, seg_col, feat_k, values, dk_intra, dv_intra, d_query,
    own_far, pair_in, other_far, q3, w0, w2, w3, own, partner,
):
    rows = w0.shape[0]
    weights = (
        (own_far[:, FAR_Q_COLUMNS], w0[...]),
        (pair_in[:rows, PAIR_Q_COLUMNS], pair_in[:rows, KV_COLUMNS]),
        (other_far[:, FAR_Q_COLUMNS], w2[...]),
        (q3[...], w3[...]),
    )
    for i in (1, 0):
        ids, total = received(-1, pair, middle, further, i)
        take = seg_col[i] == ids
        d_key, d_value = [], []
        for g in range(2):
            back = total[head(g)]
            k, v = feat_k[i, g], values[i, g]
            dk = dk_intra[i, g] + jnp.where(take, dot_nt(v, back), 0.0)
            dv = dv_intra[i, g] + jnp.where(take, dot_nn(k, back), 0.0)
            d_key.append((dk * jnp.minimum(k.astype(f32), 1.0)).astype(bf16))
            d_value.append(dv.astype(bf16))
        d_proj = jnp.concatenate(d_key + d_value, axis=1)
        for j, (q, w) in enumerate(weights):
            value = dot_nt(d_query[i], q) + dot_nt(d_proj, w)
            if i == 1:
                partner[j ^ 1] = value.astype(bf16)
            else:
                own[j] = value


def final_body(own, partner, tokens, cot, inv_rms, gain, grad, work):
    inner = None
    for j in range(4):
        at = columns(lax.axis_index("dp") ^ j, 256)
        norm_grad = (own[j] + partner[j].astype(f32)) * gain[:, at]
        work[j] = norm_grad
        part = jnp.sum(tokens[:, at].astype(f32) * norm_grad, axis=1, keepdims=True)
        inner = part if inner is None else inner + part
    inv = inv_rms[...]
    scale = inv**3 * (inner * (1.0 / D))
    for j in range(4):
        at = columns(lax.axis_index("dp") ^ j, 256)
        value = cot[:, at].astype(f32) + inv * work[j] - tokens[:, at].astype(f32) * scale
        grad[:, at] = value.astype(bf16)


def flip(array, axis, bit):
    n = lax.axis_size(axis)
    return lax.ppermute(array, axis, [(i, i ^ bit) for i in range(n)])


def shift(array, axis, step):
    n = lax.axis_size(axis)
    return lax.ppermute(array, axis, [(i, i + step) for i in range(n) if 0 <= i + step < n])


def carry(message, ends, step):
    n = lax.axis_size("seq")
    if n == 4:
        middle = lax.ppermute(message, "seq", [(1, 2), (2, 1)])
        return flip(message, "seq", 1), middle, flip(message, "seq", 2)
    position = lax.axis_index("seq")
    begin, end = (ends[0], ends[1]) if step > 0 else (ends[1], ends[0])
    total = message[:, : 2 * HEAD_DIM].astype(f32)
    reach = 1
    while reach < n:
        before = shift(total, "seq", step * reach)
        ids = shift(jnp.stack([begin, end]), "seq", step * reach)
        there = position - step * reach
        there = (there >= 0) & (there < n)
        goes_on = there & (begin == end) & (ids[1] == begin)
        total = total + jnp.where(goes_on[:, None, None], before, 0.0)
        begin = jnp.where(there, ids[0], begin)
        reach *= 2
    rows = jnp.concatenate([total.astype(bf16), message[:, 2 * HEAD_DIM :]], axis=1)
    near = shift(rows, "seq", step)
    return near, near, near


def reduce_weight(rest, a_send, b_send):
    n = lax.axis_size("seq")
    half, width = a_send.shape
    quarter = half // 2
    kept, a_send, b_send = call(
        weight_one_body,
        [((half, width), f32), ((quarter, width), bf16), ((quarter, width), bf16)],
        rest, flip(a_send, "dp", 2), flip(b_send, "seq", 1), us=W1,
    )
    outs = [((half, width), f32), ((half, width), bf16)]
    kept, send = call(weight_two_body, outs, kept, flip(a_send, "seq", 1), flip(b_send, "dp", 2), us=W2)
    reach = 2
    while reach < n:
        kept, send = call(weight_three_body, outs, kept, flip(send, "seq", reach), us=W3)
        reach *= 2
    return kept, flip(send, "seq", 1)


def shards(tokens, segment_ids, norm_gain, w_qkv, head_gain, w_out, cotangent):
    length = segment_ids.shape[1]
    width = HEADS * HEAD_DIM
    n = lax.axis_size("seq")
    flat = tokens.reshape(length, D)
    cot = cotangent.reshape(length, D)
    gain = norm_gain.reshape(1, D)
    gain_h = head_gain.reshape(1, width)
    wide = (2, 2, length, HEAD_DIM)

    kv_mine, kv_other = split(w_qkv)
    kv_x, kv_diagonal = flip(kv_mine, "dp", 2), flip(kv_other, "dp", 3)
    partner = flip(flat, "dp", 1)
    partner, w_late, out_late = lax.optimization_barrier((partner, w_qkv, w_out))
    for_pair, far_own, q_other = pack(w_late, out_late, segment_ids, kv_other)
    pair = flip(for_pair, "dp", 1)

    normed, inv_rms, seg_col, seg_row, raw_near = call(
        prep_body,
        [
            ((4, 2 * length, D // 4), bf16),
            ((length, 1), f32),
            ((2, length, HEAD_DIM), f32),
            ((2, 1, length), f32),
            ((2 * length, 4 * HEAD_DIM), f32),
        ],
        flat, partner, segment_ids, gain, kv_mine, pair, us=20.0,
    )
    kv_x, far_own, q_other = lax.optimization_barrier((kv_x, far_own, q_other))
    kv_diagonal, cot_partner = lax.optimization_barrier((kv_diagonal, flip(cot, "dp", 1)))
    far_x, q_diagonal = flip(far_own, "dp", 2), flip(q_other, "dp", 3)

    message = ((2, 2 * HEAD_DIM + ID_ROWS, HEAD_DIM), bf16)
    feat_k, values, state = call(
        kv_body, [(wide, bf16), (wide, bf16), message], raw_near, normed, kv_x, kv_diagonal, seg_col
    )
    ends = jnp.stack([seg_col[:, 0, 0], seg_col[:, -1, 0]])
    near = carry(state, ends, 1)
    feat_q, intra, upstream = call(
        query_body,
        [(wide, bf16), (wide, f32), (wide, f32)],
        normed, far_own, pair, far_x, q_diagonal, feat_k, values, seg_col, seg_row, cot, cot_partner, gain_h, us=0.1,
    )
    rows = HEAD_DIM // 2
    mixed, d_attn, back, before, rest, a_send, b_send = call(
        attn_body,
        [
            (wide, bf16),
            (wide, bf16),
            message,
            ((2, 2 * HEAD_DIM, HEAD_DIM), bf16),
            ((2 * rows, D), f32),
            ((rows, D), bf16),
            ((2, rows // 2, D), bf16),
        ],
        *near, seg_col, feat_q, intra, upstream, gain_h, cot, cot_partner,
    )
    back_near = carry(back, ends, -1)
    scale = 1.0 / math.sqrt(length * lax.axis_size("dp") * n)
    kept, arrived = reduce_weight(rest, a_send, b_send)
    d_query, dk_intra, dv_intra, out_partner = call(
        back_body,
        [((2, length, 2 * HEAD_DIM), bf16), (wide, f32), (wide, f32), ((length, D), bf16)],
        near[0], before, near[1], seg_col, seg_row, d_attn, values, feat_k, feat_q, mixed, far_own, far_x,
    )
    (output,) = call(
        output_body,
        [((length, D), bf16)],
        flat, flip(out_partner, "dp", 1), mixed, far_own, far_x,
    )
    own, theirs = call(
        project_back_body,
        [((4, length, D // 4), f32), ((4, length, D // 4), bf16)],
        *back_near, seg_col, feat_k, values, dk_intra, dv_intra, d_query,
        far_own, pair, far_x, q_diagonal, kv_mine, kv_x, kv_diagonal,
    )
    (grad,) = call(
        final_body,
        [((length, D), bf16)],
        own, flip(theirs, "dp", 1), flat, cot, inv_rms, gain,
        scratch=[((4, length, D // 4), f32)],
    )
    output, grad, kept = lax.optimization_barrier((output, grad, kept))
    (grad_out_weight,) = call(
        functools.partial(weight_last_body, scale), [((HEAD_DIM, D), f32)], kept, arrived
    )
    return (output.reshape(tokens.shape), grad.reshape(tokens.shape), grad_out_weight)


def solution(mesh):
    in_specs = (
        P(("groups", "dp"), "seq", None),
        P(("groups", "dp"), "seq"),
        P(),
        P("dp", None),
        P(),
        P("dp", None),
        P(("groups", "dp"), "seq", None),
    )
    out_specs = (
        P(("groups", "dp"), "seq", None),
        P(("groups", "dp"), "seq", None),
        P(("groups", "dp"), None),
    )
    return jax.shard_map(shards, mesh=mesh, in_specs=in_specs, out_specs=out_specs, check_vma=False)
```

```python
import functools
import math

import jax
import jax.numpy as jnp
from jax import lax
from jax.experimental import pallas as pl
from jax.experimental.pallas import tpu as pltpu
from jax.sharding import PartitionSpec as P

D = 1024
HEADS = 4
HEAD_DIM = 128
ID_ROWS = 16

epsilon = 1e-06
W1, W2, W3, PREP, QUERY, MIXED, BACK, PROJECT, SPLIT = 8.0, 8.0, 8.0, 20.0, 0.1, 0.1, 2.0, 2.0, 20.0

f32 = jnp.float32
bf16 = jnp.bfloat16


def dot_nn(a, b):
    return lax.dot_general(a, b, (((1,), (0,)), ((), ())), preferred_element_type=f32)


def dot_nt(a, b):
    return lax.dot_general(a, b, (((1,), (1,)), ((), ())), preferred_element_type=f32)


def dot_tn(a, b):
    return lax.dot_general(a, b, (((0,), (0,)), ((), ())), preferred_element_type=f32)


def feature_map(u):
    return jnp.where(u > 0, u + 1.0, jnp.exp(jnp.minimum(u, 0.0)))


def head(h):
    return slice(h * HEAD_DIM, (h + 1) * HEAD_DIM)


VMEM = pl.BlockSpec(memory_space=pltpu.VMEM)
ANY = pl.BlockSpec(memory_space=pl.ANY)


def call(body, outs, *args, scratch=(), us=2.0):
    return pl.pallas_call(
        body,
        out_shape=[jax.ShapeDtypeStruct(shape, dtype) for shape, dtype in outs],
        in_specs=[VMEM] * len(args),
        out_specs=[VMEM] * len(outs),
        scratch_shapes=[pltpu.VMEM(shape, dtype) for shape, dtype in scratch],
        compiler_params=pltpu.CompilerParams(vmem_limit_bytes=16 * 1024 * 1024),
        cost_estimate=pl.CostEstimate(flops=int(us * 1e9), transcendentals=0, bytes_accessed=int(us * 3e6)),
    )(*args)


def columns(index, width):
    return pl.ds(pl.multiple_of(index * width, width), width)


def causal(seg_col, seg_row, i):
    length = seg_row.shape[2]
    order = lax.broadcasted_iota(jnp.int32, (length, length), 0) >= lax.broadcasted_iota(
        jnp.int32, (length, length), 1
    )
    down = jnp.concatenate([seg_col[i]] * (length // HEAD_DIM), axis=1)
    return (down == seg_row[i]) & order


def run_all(copies, sem):
    copies = [pltpu.make_async_copy(source, target, sem.at[n]) for n, (source, target) in enumerate(copies)]
    for copy in copies:
        copy.start()
    for copy in copies:
        copy.wait()


def kv_columns(n, which):
    return columns(4 + 4 * (n // 2) + 2 * (n % 2) + which, HEAD_DIM)


def split_half_body(w, half, sem):
    c, rows = lax.axis_index("dp") % 2, half.shape[0]
    part = pl.ds(pl.multiple_of(lax.axis_index("groups") * rows, rows), rows)
    run_all([(w.at[part, kv_columns(n, 1 - c)], half.at[:, head(n)]) for n in range(4)], sem)


def split_kv_body(w, seg, _, mine, other, sem):
    c = lax.axis_index("dp") % 2
    rows, length = w.shape[0], seg.shape[1]
    other[rows:, :length] = jnp.broadcast_to(seg[...].astype(f32), (ID_ROWS, length)).astype(bf16)
    copies = []
    for target, which in ((mine, c), (other, 1 - c)):
        copies += [(w.at[:, kv_columns(n, which)], target.at[:rows, head(n)]) for n in range(4)]
    run_all(copies, sem)


def split_q_body(w, w_out, far, other, sem):
    c = lax.axis_index("dp") % 2
    rows, half = w_out.shape[0], w_out.shape[1] // 2
    copies = [
        (w_out.at[:, :half], far.at[:rows, 2 * HEAD_DIM :]),
        (w_out.at[:, half:], far.at[rows:, 2 * HEAD_DIM :]),
    ]
    for target, which in ((far, c), (other, 1 - c)):
        copies += [(w.at[:, columns(2 * g + which, HEAD_DIM)], target.at[:, head(g)]) for g in range(2)]
    run_all(copies, sem)


def split(body, shapes, copies, us, w, *rest, specs=()):
    return pl.pallas_call(
        body,
        out_shape=[jax.ShapeDtypeStruct(shape, bf16) for shape in shapes],
        in_specs=[ANY, *specs],
        out_specs=[VMEM] * len(shapes),
        scratch_shapes=[pltpu.SemaphoreType.DMA((copies,))],
        compiler_params=pltpu.CompilerParams(vmem_limit_bytes=8 * 1024 * 1024),
        cost_estimate=pl.CostEstimate(flops=int(us * 1e9), transcendentals=0, bytes_accessed=10**6),
    )(w, *rest)


FAR_Q = slice(0, 2 * HEAD_DIM)


def out_rows(far):
    rows = far.shape[0] // 2
    return far[:rows, 2 * HEAD_DIM :], far[rows:, 2 * HEAD_DIM :]


def halves():
    at = lax.axis_index("groups")
    return at, 1 - at


def sources(step):
    at, n = lax.axis_index("seq"), lax.axis_size("seq")
    if n != 4:
        return at < 0, at < 0
    return (at % 2 == 1, at >= 2) if step > 0 else (at % 2 == 0, at < 2)


def prep_body(tokens, partner, seg, gain, w0, w1, normed, inv_rms, seg_col, seg_row, raw):
    length = seg.shape[1]
    for i, (part, ids) in enumerate(((tokens, seg[...].astype(f32)), (partner, w1[w0.shape[0] : w0.shape[0] + 1, :length].astype(f32)))):
        x = part[...].astype(f32)
        inv = lax.rsqrt(jnp.mean(x * x, axis=1, keepdims=True) + epsilon)
        if i == 0:
            inv_rms[...] = inv
        for j in range(4):
            at = columns(lax.axis_index("dp") ^ j, 256)
            normed[j, i * length : (i + 1) * length] = (part[:, at].astype(f32) * inv * gain[:, at]).astype(bf16)
        seg_row[i] = ids
        seg_col[i] = jnp.broadcast_to(ids, (HEAD_DIM, length)).T
    rows = w0.shape[0]
    raw[...] = dot_nn(normed[0], w0[...]) + dot_nn(normed[1], w1[:rows])


def store_state(state, state_far, i, g, value):
    for target in (state, state_far):
        target[i, head(g), :] = value.astype(bf16)


def store_ids(state, state_far, i, ids):
    for target in (state, state_far):
        rows = target.shape[1] - 2 * HEAD_DIM
        target[i, 2 * HEAD_DIM :, :] = jnp.broadcast_to(ids, (rows, HEAD_DIM)).astype(bf16)


def kv_body(near, normed, w2, w3, w3_other, seg_col, feat_k, values, state, state_far):
    raw = near[...] + dot_nn(normed[2], w2[...])
    for at, w in zip(halves(), (w3, w3_other)):
        raw += dot_nn(normed[3, :, columns(at, w.shape[0])], w[...])
    raw = raw.astype(bf16)
    length = seg_col.shape[1]
    for i in range(2):
        last = seg_col[i, length - 1 : length, :]
        tail = seg_col[i] == last
        rows = slice(i * length, (i + 1) * length)
        for g in range(2):
            k = feature_map(raw[rows, head(g)].astype(f32))
            v = raw[rows, head(2 + g)]
            feat_k[i, g] = k.astype(bf16)
            values[i, g] = v
            store_state(state, state_far, i, g, dot_tn(jnp.where(tail, k, 0.0).astype(bf16), v))
        store_ids(state, state_far, i, last)


def query_body(normed, w0, w1, w2, w3, feat_k, values, seg_col, seg_row, feat_q, intra):
    raw = dot_nn(normed[0], w0[:, FAR_Q]) + dot_nn(normed[1], w1[...])
    raw += dot_nn(normed[2], w2[:, FAR_Q]) + dot_nn(normed[3], w3[...])
    raw = raw.astype(bf16)
    length = seg_row.shape[2]
    for i in range(2):
        mask = causal(seg_col, seg_row, i)
        for g in range(2):
            q = feature_map(raw[i * length : (i + 1) * length, head(g)].astype(f32)).astype(bf16)
            feat_q[i, g] = q
            s = jnp.where(mask, dot_nt(q, feat_k[i, g]), 0.0).astype(bf16)
            intra[i, g] = dot_nn(s, values[i, g])


def mixed_grad_body(cot, cot_partner, own, other, gain, upstream):
    for j, o in enumerate((own, other)):
        full = lax.axis_index("dp") ^ (2 * j)
        for i, part in enumerate((cot, cot_partner)):
            value = sum(dot_nt(part[:, n * 512 : (n + 1) * 512], half) for n, half in enumerate(out_rows(o)))
            upstream[i, full // 2] = value * gain[:, columns(full, HEAD_DIM)]


def received(step, pair, middle, further, i):
    use_pair, use_further = sources(step)
    near = jnp.where(use_pair, pair[i].astype(f32), middle[i].astype(f32))
    ids = near[2 * HEAD_DIM : 2 * HEAD_DIM + 1, :]
    far = further[i].astype(f32)
    same = (far[2 * HEAD_DIM : 2 * HEAD_DIM + 1, :] == ids) & use_further
    total = near[: 2 * HEAD_DIM] + jnp.where(same, far[: 2 * HEAD_DIM], 0.0)
    return ids, total.astype(bf16)


def attn_body(
    pair, middle, further, seg_col, feat_q, intra, upstream, gain, cot, cot_partner,
    mixed, d_attn, state, state_far, before, rest, a_send, b_send,
):
    for i in range(2):
        first = seg_col[i, 0:1, :]
        begin = seg_col[i] == first
        ids, total = received(1, pair, middle, further, i)
        before[i] = total
        take = seg_col[i] == ids
        for g in range(2):
            q = feat_q[i, g]
            attention = intra[i, g] + jnp.where(take, dot_nn(q, total[head(g)]), 0.0)
            ratio = lax.rsqrt(jnp.mean(attention * attention, axis=1, keepdims=True) + epsilon)
            mixed[i, g] = (attention * ratio * gain[:, columns(2 * g + lax.axis_index("dp") % 2, HEAD_DIM)]).astype(bf16)
            up = upstream[i, g]
            inner = jnp.mean(attention * up, axis=1, keepdims=True)
            da = (ratio * up - ratio**3 * attention * inner).astype(bf16)
            d_attn[i, g] = da
            store_state(state, state_far, i, g, dot_tn(jnp.where(begin, q.astype(f32), 0.0).astype(bf16), da))
        store_ids(state, state_far, i, first)
    half = HEAD_DIM // 2
    quarter = half // 2
    second = lax.axis_index("seq") % 2 == 1
    for j in range(2):
        g = (lax.axis_index("dp") ^ (2 * j)) // 2
        part = dot_tn(mixed[0, g], cot[...]) + dot_tn(mixed[1, g], cot_partner[...])
        if j == 0:
            rest[:half] = part[:half]
        else:
            a_send[...] = part[:half].astype(bf16)
        low, high = part[half : half + quarter], part[half + quarter :]
        rest[half + j * quarter : half + (j + 1) * quarter] = jnp.where(second, high, low)
        b_send[j] = jnp.where(second, low, high).astype(bf16)


def weight_one_body(rest, a_in, b_in, kept, a_send, b_send):
    second = lax.axis_index("seq") % 2 == 1
    quarter = b_in.shape[1]
    low = rest[:quarter] + a_in[:quarter].astype(f32)
    high = rest[quarter : 2 * quarter] + a_in[quarter:].astype(f32)
    kept[:quarter] = jnp.where(second, high, low)
    a_send[...] = jnp.where(second, low, high).astype(bf16)
    kept[quarter:] = rest[2 * quarter : 3 * quarter] + b_in[0].astype(f32)
    b_send[...] = (rest[3 * quarter :] + b_in[1].astype(f32)).astype(bf16)


def weight_two_body(kept, a_in, b_in, total, send):
    quarter = a_in.shape[0]
    total[:quarter] = kept[:quarter] + a_in[...].astype(f32)
    total[quarter:] = kept[quarter:] + b_in[...].astype(f32)
    send[...] = total[...].astype(bf16)


def weight_three_body(kept, arrived, total, send):
    total[...] = kept[...] + arrived[...].astype(f32)
    send[...] = total[...].astype(bf16)


def weight_last_body(scale, kept, arrived, grad):
    quarter = kept.shape[0] // 2
    second = lax.axis_index("seq") % 2 == 1
    mine, theirs = kept[...] * scale, arrived[...].astype(f32) * scale
    low = jnp.where(second, theirs, mine)
    high = jnp.where(second, mine, theirs)
    for n, part in enumerate((low[:quarter], high[:quarter], low[quarter:], high[quarter:])):
        grad[n * quarter : (n + 1) * quarter] = part


def back_body(
    pair, before, middle, seg_col, seg_row, d_attn, values, feat_k, feat_q,
    d_query, dk_intra, dv_intra,
):
    for i in range(2):
        mask = causal(seg_col, seg_row, i)
        use_pair, _ = sources(1)
        last = 2 * HEAD_DIM
        ids = jnp.where(use_pair, pair[i, last : last + 1].astype(f32), middle[i, last : last + 1].astype(f32))
        take = seg_col[i] == ids
        for g in range(2):
            da, q, k = d_attn[i, g], feat_q[i, g], feat_k[i, g]
            s = jnp.where(mask, dot_nt(q, k), 0.0).astype(bf16)
            ds = jnp.where(mask, dot_nt(da, values[i, g]), 0.0).astype(bf16)
            dq = dot_nn(ds, k) + jnp.where(take, dot_nt(da, before[i, head(g)]), 0.0)
            d_query[i, :, head(g)] = (dq * jnp.minimum(q.astype(f32), 1.0)).astype(bf16)
            dk_intra[i, g] = dot_tn(ds, q)
            dv_intra[i, g] = dot_tn(s, da)


def output_body(tokens, partner, mixed, own, other, output):
    x = lax.axis_index("dp") // 2
    for n, (a, b) in enumerate(zip(out_rows(own), out_rows(other))):
        at = slice(n * 512, (n + 1) * 512)
        total = dot_nn(mixed[0, x], a) + dot_nn(mixed[0, 1 - x], b)
        output[:, at] = (tokens[:, at].astype(f32) + (total + partner[:, at].astype(f32))).astype(bf16)


def project_back_body(
    pair, middle, further, seg_col, feat_k, values, dk_intra, dv_intra, d_query,
    q0, q1, q2, q3, w0, w1, w2, w3, w3_other, mixed, own, partner, out_partner, work,
):
    x = lax.axis_index("dp") // 2
    for n, (a, b) in enumerate(zip(out_rows(q0), out_rows(q2))):
        out_partner[:, n * 512 : (n + 1) * 512] = (dot_nn(mixed[1, x], a) + dot_nn(mixed[1, 1 - x], b)).astype(bf16)
    rows = w0.shape[0]
    q = (q0[:, FAR_Q], q1[...], q2[:, FAR_Q], q3[...])
    w = (w0[...], w1[:rows], w2[...])
    for i in (1, 0):
        ids, total = received(-1, pair, middle, further, i)
        take = seg_col[i] == ids
        d_key, d_value = [], []
        for g in range(2):
            back = total[head(g)]
            k, v = feat_k[i, g], values[i, g]
            dk = dk_intra[i, g] + jnp.where(take, dot_nt(v, back), 0.0)
            dv = dv_intra[i, g] + jnp.where(take, dot_nn(k, back), 0.0)
            d_key.append((dk * jnp.minimum(k.astype(f32), 1.0)).astype(bf16))
            d_value.append(dv.astype(bf16))
        d_proj = jnp.concatenate(d_key + d_value, axis=1)
        pieces = [(j, slice(None), dot_nt(d_proj, w[j])) for j in range(3)]
        pieces += [
            (3, columns(at, part.shape[0]), dot_nt(d_proj, part[...])) for at, part in zip(halves(), (w3, w3_other))
        ]
        for j in range(4):
            from_q = dot_nt(d_query[i], q[j])
            if i == 1:
                work[j ^ 1] = from_q
            else:
                own[j] = from_q
        for j, at, value in pieces:
            if i == 1:
                partner[j ^ 1, :, at] = (work[j ^ 1, :, at] + value).astype(bf16)
            else:
                own[j, :, at] += value


def final_body(own, partner, tokens, cot, inv_rms, gain, grad, work):
    inner = None
    for j in range(4):
        at = columns(lax.axis_index("dp") ^ j, 256)
        norm_grad = (own[j] + partner[j].astype(f32)) * gain[:, at]
        work[j] = norm_grad
        part = jnp.sum(tokens[:, at].astype(f32) * norm_grad, axis=1, keepdims=True)
        inner = part if inner is None else inner + part
    inv = inv_rms[...]
    scale = inv**3 * (inner * (1.0 / D))
    for j in range(4):
        at = columns(lax.axis_index("dp") ^ j, 256)
        value = cot[:, at].astype(f32) + inv * work[j] - tokens[:, at].astype(f32) * scale
        grad[:, at] = value.astype(bf16)


def flip(array, axis, bit):
    n = lax.axis_size(axis)
    return lax.ppermute(array, axis, [(i, i ^ bit) for i in range(n)])


def shift(array, axis, step):
    n = lax.axis_size(axis)
    return lax.ppermute(array, axis, [(i, i + step) for i in range(n) if 0 <= i + step < n])


def carry(message, longer, ends, step, late=None):
    n = lax.axis_size("seq")
    if n == 4:
        middle = lax.ppermute(message, "seq", [(1, 2), (2, 1)])
        return flip(message if late is None else late, "seq", 1), middle, flip(longer, "seq", 2)
    position = lax.axis_index("seq")
    begin, end = (ends[0], ends[1]) if step > 0 else (ends[1], ends[0])
    total = message[:, : 2 * HEAD_DIM].astype(f32)
    reach = 1
    while reach < n:
        before = shift(total, "seq", step * reach)
        ids = shift(jnp.stack([begin, end]), "seq", step * reach)
        there = position - step * reach
        there = (there >= 0) & (there < n)
        goes_on = there & (begin == end) & (ids[1] == begin)
        total = total + jnp.where(goes_on[:, None, None], before, 0.0)
        begin = jnp.where(there, ids[0], begin)
        reach *= 2
    rows = jnp.concatenate([total.astype(bf16), message[:, 2 * HEAD_DIM :]], axis=1)
    near = shift(rows, "seq", step)
    return near, near, near


def reduce_weight(rest, a_send, b_send, back, ends, d_attn):
    n = lax.axis_size("seq")
    half, width = a_send.shape
    quarter = half // 2
    kept, a_send, b_send = call(
        weight_one_body,
        [((half, width), f32), ((quarter, width), bf16), ((quarter, width), bf16)],
        rest, flip(a_send, "dp", 2), flip(b_send, "seq", 1), us=W1,
    )
    a_send, back_late = lax.optimization_barrier((a_send, back[0]))
    back_near = carry(back[0], back[1], ends, -1, back_late)
    outs = [((half, width), f32), ((half, width), bf16)]
    kept, send = call(weight_two_body, outs, kept, flip(a_send, "seq", 1), flip(b_send, "dp", 2), us=W2)
    reach = 2
    while reach < n:
        kept, send = call(weight_three_body, outs, kept, flip(send, "seq", reach), us=W3)
        reach *= 2
    return kept, flip(send, "seq", 1), back_near, d_attn


def shards(tokens, segment_ids, norm_gain, w_qkv, head_gain, w_out, cotangent):
    length = segment_ids.shape[1]
    width = HEADS * HEAD_DIM
    n = lax.axis_size("seq")
    flat = tokens.reshape(length, D)
    cot = cotangent.reshape(length, D)
    gain = norm_gain.reshape(1, D)
    gain_h = head_gain.reshape(1, width)
    wide = (2, 2, length, HEAD_DIM)

    shard_rows = w_qkv.shape[0]
    (kv_half,) = split(split_half_body, [(shard_rows // 2, 4 * HEAD_DIM)], 4, 1.0, w_qkv)
    kv_diagonal = flip(kv_half, "dp", 3)
    kv_mine, kv_other = split(
        split_kv_body,
        [(shard_rows, 4 * HEAD_DIM), (shard_rows + ID_ROWS, 4 * HEAD_DIM)],
        8, SPLIT, w_qkv, segment_ids, kv_half, specs=(VMEM, ANY),
    )
    kv_x, kv_pair = flip(kv_mine, "dp", 2), flip(kv_other, "dp", 1)
    partner, cot_partner = flip(flat, "dp", 1), flip(cot, "dp", 1)
    partner, kv_pair, cot_partner, w_late = lax.optimization_barrier((partner, kv_pair, cot_partner, w_qkv))
    normed, inv_rms, seg_col, seg_row, raw_near = call(
        prep_body,
        [
            ((4, 2 * length, D // 4), bf16),
            ((length, 1), f32),
            ((2, length, HEAD_DIM), f32),
            ((2, 1, length), f32),
            ((2 * length, 4 * HEAD_DIM), f32),
        ],
        flat, partner, segment_ids, gain, kv_mine, kv_pair, us=PREP,
    )
    far_own, q_other = split(
        split_q_body, [(shard_rows, 6 * HEAD_DIM), (shard_rows, 2 * HEAD_DIM)], 6, 1.0, w_late, w_out, specs=(ANY,)
    )
    kv_diagonal, inv_rms, far_own, q_other = lax.optimization_barrier((kv_diagonal, inv_rms, far_own, q_other))
    kv_diagonal_other = flip(kv_diagonal, "groups", 1)
    far_x = flip(far_own, "dp", 2)
    kv_x, q_pair = lax.optimization_barrier((kv_x, flip(q_other, "dp", 1)))
    wq = [far_own, q_pair, far_x, flip(q_other, "dp", 3)]
    kv = [kv_mine, kv_pair, kv_x, kv_diagonal, kv_diagonal_other]
    out = [far_own, far_x]

    message = ((2, 2 * HEAD_DIM + ID_ROWS, HEAD_DIM), bf16)
    longer = ((2, 2 * HEAD_DIM + 2 * ID_ROWS, HEAD_DIM), bf16)
    feat_k, values, state, state_far = call(
        kv_body, [(wide, bf16), (wide, bf16), message, longer], raw_near, normed, *kv[2:], seg_col
    )
    ends = jnp.stack([seg_col[:, 0, 0], seg_col[:, -1, 0]])
    near = carry(state, state_far, ends, 1)
    (upstream,) = call(
        mixed_grad_body, [(wide, f32)], cot, cot_partner, *out, gain_h, us=MIXED
    )
    upstream, feat_k, feat_k_late = lax.optimization_barrier((upstream, feat_k, feat_k))
    feat_q, intra = call(
        query_body, [(wide, bf16), (wide, f32)], normed, *wq, feat_k_late, values, seg_col, seg_row, us=QUERY
    )
    rows = HEAD_DIM // 2
    mixed, d_attn, back, back_far, before, rest, a_send, b_send = call(
        attn_body,
        [
            (wide, bf16),
            (wide, bf16),
            message,
            longer,
            ((2, 2 * HEAD_DIM, HEAD_DIM), bf16),
            ((2 * rows, D), f32),
            ((rows, D), bf16),
            ((2, rows // 2, D), bf16),
        ],
        *near, seg_col, feat_q, intra, upstream, gain_h, cot, cot_partner,
    )
    scale = 1.0 / math.sqrt(length * lax.axis_size("dp") * n)
    kept, arrived, back_near, d_attn = reduce_weight(rest, a_send, b_send, (back, back_far), ends, d_attn)
    d_query, dk_intra, dv_intra = call(
        back_body,
        [((2, length, 2 * HEAD_DIM), bf16), (wide, f32), (wide, f32)],
        near[0], before, near[1], seg_col, seg_row, d_attn, values, feat_k, feat_q, us=BACK,
    )
    own, theirs, out_partner = call(
        project_back_body,
        [((4, length, D // 4), f32), ((4, length, D // 4), bf16), ((length, D), bf16)],
        *back_near, seg_col, feat_k, values, dk_intra, dv_intra, d_query,
        *wq, *kv, mixed, us=PROJECT, scratch=[((4, length, D // 4), f32)],
    )
    (output,) = call(
        output_body,
        [((length, D), bf16)],
        flat, flip(out_partner, "dp", 1), mixed, *out,
    )
    (grad,) = call(
        final_body,
        [((length, D), bf16)],
        own, flip(theirs, "dp", 1), flat, cot, inv_rms, gain,
        scratch=[((4, length, D // 4), f32)],
    )
    output, grad, kept = lax.optimization_barrier((output, grad, kept))
    (grad_out_weight,) = call(
        functools.partial(weight_last_body, scale), [((HEAD_DIM, D), f32)], kept, arrived
    )
    return (output.reshape(tokens.shape), grad.reshape(tokens.shape), grad_out_weight)


def solution(mesh):
    in_specs = (
        P(("groups", "dp"), "seq", None),
        P(("groups", "dp"), "seq"),
        P(),
        P("dp", None),
        P(),
        P("dp", None),
        P(("groups", "dp"), "seq", None),
    )
    out_specs = (
        P(("groups", "dp"), "seq", None),
        P(("groups", "dp"), "seq", None),
        P(("groups", "dp"), None),
    )
    return jax.shard_map(shards, mesh=mesh, in_specs=in_specs, out_specs=out_specs, check_vma=False)
```

```python
import functools
import math

import jax
import jax.numpy as jnp
from jax import lax
from jax.experimental import pallas as pl
from jax.experimental.pallas import tpu as pltpu
from jax.sharding import PartitionSpec as P

D = 1024
HEADS = 4
HEAD_DIM = 128
ID_ROWS = 16

epsilon = 1e-06
W1, W2, W3, PREP, QUERY, MIXED, BACK, PROJECT, SPLIT, FILL = 8.0, 8.0, 8.0, 20.0, 0.5, 0.1, 0.1, 2.0, 20.0, 2.0

f32 = jnp.float32
bf16 = jnp.bfloat16


def dot_nn(a, b):
    return lax.dot_general(a, b, (((1,), (0,)), ((), ())), preferred_element_type=f32)


def dot_nt(a, b):
    return lax.dot_general(a, b, (((1,), (1,)), ((), ())), preferred_element_type=f32)


def dot_tn(a, b):
    return lax.dot_general(a, b, (((0,), (0,)), ((), ())), preferred_element_type=f32)


def feature_map(u):
    return jnp.where(u > 0, u + 1.0, jnp.exp(jnp.minimum(u, 0.0)))


def head(h):
    return slice(h * HEAD_DIM, (h + 1) * HEAD_DIM)


VMEM = pl.BlockSpec(memory_space=pltpu.VMEM)
ANY = pl.BlockSpec(memory_space=pl.ANY)


def call(body, outs, *args, scratch=(), us=2.0):
    return pl.pallas_call(
        body,
        out_shape=[jax.ShapeDtypeStruct(shape, dtype) for shape, dtype in outs],
        in_specs=[VMEM] * len(args),
        out_specs=[VMEM] * len(outs),
        scratch_shapes=[pltpu.VMEM(shape, dtype) for shape, dtype in scratch],
        compiler_params=pltpu.CompilerParams(vmem_limit_bytes=16 * 1024 * 1024),
        cost_estimate=pl.CostEstimate(flops=int(us * 1e9), transcendentals=0, bytes_accessed=int(us * 3e6)),
    )(*args)


def columns(index, width):
    return pl.ds(pl.multiple_of(index * width, width), width)


def causal(seg_col, seg_row, i):
    length = seg_row.shape[2]
    order = lax.broadcasted_iota(jnp.int32, (length, length), 0) >= lax.broadcasted_iota(
        jnp.int32, (length, length), 1
    )
    down = jnp.concatenate([seg_col[i]] * (length // HEAD_DIM), axis=1)
    return (down == seg_row[i]) & order


def run_all(copies, sem):
    copies = [pltpu.make_async_copy(source, target, sem.at[n]) for n, (source, target) in enumerate(copies)]
    for copy in copies:
        copy.start()
    for copy in copies:
        copy.wait()


def kv_columns(n, which):
    return columns(4 + 4 * (n // 2) + 2 * (n % 2) + which, HEAD_DIM)


def split_half_body(w, half, sem):
    c, rows = lax.axis_index("dp") % 2, half.shape[0]
    part = pl.ds(pl.multiple_of(lax.axis_index("groups") * rows, rows), rows)
    run_all([(w.at[part, kv_columns(n, 1 - c)], half.at[:, head(n)]) for n in range(4)], sem)


def split_kv_body(w, seg, _, mine, other, sem):
    c = lax.axis_index("dp") % 2
    rows, length = w.shape[0], seg.shape[1]
    other[rows:, :length] = jnp.broadcast_to(seg[...].astype(f32), (ID_ROWS, length)).astype(bf16)
    copies = []
    for target, which in ((mine, c), (other, 1 - c)):
        copies += [(w.at[:, kv_columns(n, which)], target.at[:rows, head(n)]) for n in range(4)]
    copies += [(w.at[:, columns(2 * g + 1 - c, HEAD_DIM)], other.at[:rows, head(4 + g)]) for g in range(2)]
    run_all(copies, sem)


def split_q_body(w, mine, other, sem):
    c = lax.axis_index("dp") % 2
    copies = []
    for target, which in ((mine, c), (other, 1 - c)):
        copies += [(w.at[:, columns(2 * g + which, HEAD_DIM)], target.at[:, head(g)]) for g in range(2)]
    run_all(copies, sem)


def split(body, shapes, copies, us, w, *rest, specs=()):
    return pl.pallas_call(
        body,
        out_shape=[jax.ShapeDtypeStruct(shape, bf16) for shape in shapes],
        in_specs=[ANY, *specs],
        out_specs=[VMEM] * len(shapes),
        scratch_shapes=[pltpu.SemaphoreType.DMA((copies,))],
        compiler_params=pltpu.CompilerParams(vmem_limit_bytes=8 * 1024 * 1024),
        cost_estimate=pl.CostEstimate(flops=int(us * 1e9), transcendentals=0, bytes_accessed=10**6),
    )(w, *rest)


KV_COLUMNS = slice(0, 4 * HEAD_DIM)
PAIR_Q = slice(4 * HEAD_DIM, 6 * HEAD_DIM)


def halves():
    at = lax.axis_index("groups")
    return at, 1 - at


def sources(step):
    at, n = lax.axis_index("seq"), lax.axis_size("seq")
    if n != 4:
        return at < 0, at < 0
    return (at % 2 == 1, at >= 2) if step > 0 else (at % 2 == 0, at < 2)


def prep_body(tokens, partner, gain, w0, normed, inv_rms, raw):
    length = tokens.shape[0]
    for i, part in enumerate((tokens, partner)):
        x = part[...].astype(f32)
        inv = lax.rsqrt(jnp.mean(x * x, axis=1, keepdims=True) + epsilon)
        if i == 0:
            inv_rms[...] = inv
        for j in range(4):
            at = columns(lax.axis_index("dp") ^ j, 256)
            normed[j, i * length : (i + 1) * length] = (part[:, at].astype(f32) * inv * gain[:, at]).astype(bf16)
    raw[...] = dot_nn(normed[0], w0[...])


def store_state(targets, i, g, value):
    for target in targets:
        target[i, head(g), :] = value.astype(bf16)


def store_ids(targets, i, ids):
    for target in targets:
        rows = target.shape[1] - 2 * HEAD_DIM
        target[i, 2 * HEAD_DIM :, :] = jnp.broadcast_to(ids, (rows, HEAD_DIM)).astype(bf16)


def kv_body(near, normed, seg, w1, w2, w3, w3_other, feat_k, values, state, state_mid, state_far, seg_col, seg_row):
    shard_rows, length = w2.shape[0], seg.shape[1]
    for i, ids in enumerate((seg[...].astype(f32), w1[shard_rows : shard_rows + 1, :length].astype(f32))):
        seg_row[i] = ids
        seg_col[i] = jnp.broadcast_to(ids, (HEAD_DIM, length)).T
    raw = near[...] + dot_nn(normed[1], w1[:shard_rows, KV_COLUMNS]) + dot_nn(normed[2], w2[...])
    for at, w in zip(halves(), (w3, w3_other)):
        raw += dot_nn(normed[3, :, columns(at, w.shape[0])], w[...])
    raw = raw.astype(bf16)
    for i in range(2):
        last = seg_col[i, length - 1 : length, :]
        tail = seg_col[i] == last
        rows = slice(i * length, (i + 1) * length)
        for g in range(2):
            k = feature_map(raw[rows, head(g)].astype(f32))
            v = raw[rows, head(2 + g)]
            feat_k[i, g] = k.astype(bf16)
            values[i, g] = v
            store_state((state, state_mid, state_far), i, g, dot_tn(jnp.where(tail, k, 0.0).astype(bf16), v))
        store_ids((state, state_mid, state_far), i, last)


def query_body(normed, w0, w1, w2, w3, feat_k, values, seg_col, seg_row, feat_q, intra):
    raw = dot_nn(normed[0], w0[...]) + dot_nn(normed[1], w1[: w0.shape[0], PAIR_Q])
    raw += dot_nn(normed[2], w2[...]) + dot_nn(normed[3], w3[...])
    raw = raw.astype(bf16)
    length = seg_row.shape[2]
    for i in range(2):
        mask = causal(seg_col, seg_row, i)
        for g in range(2):
            q = feature_map(raw[i * length : (i + 1) * length, head(g)].astype(f32)).astype(bf16)
            feat_q[i, g] = q
            s = jnp.where(mask, dot_nt(q, feat_k[i, g]), 0.0).astype(bf16)
            intra[i, g] = dot_nn(s, values[i, g])


def mixed_grad_body(cot, cot_partner, own, other, gain, upstream):
    for j, o in enumerate((own, other)):
        full = lax.axis_index("dp") ^ (2 * j)
        for i, part in enumerate((cot, cot_partner)):
            upstream[i, full // 2] = dot_nt(part[...], o[...]) * gain[:, columns(full, HEAD_DIM)]


def received(step, pair, middle, further, i):
    use_pair, use_further = sources(step)
    used = 2 * HEAD_DIM + ID_ROWS
    near = jnp.where(use_pair, pair[i, :used].astype(f32), middle[i, :used].astype(f32))
    ids = near[2 * HEAD_DIM : 2 * HEAD_DIM + 1, :]
    far = further[i, :used].astype(f32)
    same = (far[2 * HEAD_DIM : 2 * HEAD_DIM + 1, :] == ids) & use_further
    total = near[: 2 * HEAD_DIM] + jnp.where(same, far[: 2 * HEAD_DIM], 0.0)
    return ids, total.astype(bf16)


def attn_body(
    pair, middle, further, seg_col, feat_q, intra, upstream, gain, cot, cot_partner,
    mixed, d_attn, state, state_mid, state_far, before, rest, a_send, b_send,
):
    for i in range(2):
        first = seg_col[i, 0:1, :]
        begin = seg_col[i] == first
        ids, total = received(1, pair, middle, further, i)
        before[i] = total
        take = seg_col[i] == ids
        for g in range(2):
            q = feat_q[i, g]
            attention = intra[i, g] + jnp.where(take, dot_nn(q, total[head(g)]), 0.0)
            ratio = lax.rsqrt(jnp.mean(attention * attention, axis=1, keepdims=True) + epsilon)
            mixed[i, g] = (attention * ratio * gain[:, columns(2 * g + lax.axis_index("dp") % 2, HEAD_DIM)]).astype(bf16)
            up = upstream[i, g]
            inner = jnp.mean(attention * up, axis=1, keepdims=True)
            da = (ratio * up - ratio**3 * attention * inner).astype(bf16)
            d_attn[i, g] = da
            store_state((state, state_mid, state_far), i, g, dot_tn(jnp.where(begin, q.astype(f32), 0.0).astype(bf16), da))
        store_ids((state, state_mid, state_far), i, first)
    half = HEAD_DIM // 2
    quarter = half // 2
    second = lax.axis_index("seq") % 2 == 1
    for j in range(2):
        g = (lax.axis_index("dp") ^ (2 * j)) // 2
        part = dot_tn(mixed[0, g], cot[...]) + dot_tn(mixed[1, g], cot_partner[...])
        if j == 0:
            rest[:half] = part[:half]
        else:
            a_send[...] = part[:half].astype(bf16)
        low, high = part[half : half + quarter], part[half + quarter :]
        rest[half + j * quarter : half + (j + 1) * quarter] = jnp.where(second, high, low)
        b_send[j] = jnp.where(second, low, high).astype(bf16)


def weight_one_body(rest, a_in, b_in, kept, a_send, b_send):
    second = lax.axis_index("seq") % 2 == 1
    quarter = b_in.shape[1]
    low = rest[:quarter] + a_in[:quarter].astype(f32)
    high = rest[quarter : 2 * quarter] + a_in[quarter:].astype(f32)
    kept[:quarter] = jnp.where(second, high, low)
    a_send[...] = jnp.where(second, low, high).astype(bf16)
    kept[quarter:] = rest[2 * quarter : 3 * quarter] + b_in[0].astype(f32)
    b_send[...] = (rest[3 * quarter :] + b_in[1].astype(f32)).astype(bf16)


def weight_two_body(kept, a_in, b_in, total, send):
    quarter = a_in.shape[0]
    total[:quarter] = kept[:quarter] + a_in[...].astype(f32)
    total[quarter:] = kept[quarter:] + b_in[...].astype(f32)
    send[...] = total[...].astype(bf16)


def weight_three_body(kept, arrived, total, send):
    total[...] = kept[...] + arrived[...].astype(f32)
    send[...] = total[...].astype(bf16)


def weight_last_body(scale, kept, arrived, grad):
    quarter = kept.shape[0] // 2
    second = lax.axis_index("seq") % 2 == 1
    mine, theirs = kept[...] * scale, arrived[...].astype(f32) * scale
    low = jnp.where(second, theirs, mine)
    high = jnp.where(second, mine, theirs)
    for n, part in enumerate((low[:quarter], high[:quarter], low[quarter:], high[quarter:])):
        grad[n * quarter : (n + 1) * quarter] = part


def back_body(
    pair, before, middle, seg_col, seg_row, d_attn, values, feat_k, feat_q,
    d_query, dk_intra, dv_intra,
):
    for i in range(2):
        mask = causal(seg_col, seg_row, i)
        use_pair, _ = sources(1)
        last = 2 * HEAD_DIM
        ids = jnp.where(use_pair, pair[i, last : last + 1].astype(f32), middle[i, last : last + 1].astype(f32))
        take = seg_col[i] == ids
        for g in range(2):
            da, q, k = d_attn[i, g], feat_q[i, g], feat_k[i, g]
            s = jnp.where(mask, dot_nt(q, k), 0.0).astype(bf16)
            ds = jnp.where(mask, dot_nt(da, values[i, g]), 0.0).astype(bf16)
            dq = dot_nn(ds, k) + jnp.where(take, dot_nt(da, before[i, head(g)]), 0.0)
            d_query[i, :, head(g)] = (dq * jnp.minimum(q.astype(f32), 1.0)).astype(bf16)
            dk_intra[i, g] = dot_tn(ds, q)
            dv_intra[i, g] = dot_tn(s, da)


def partner_output_body(mixed, own, other, out_partner):
    x = lax.axis_index("dp") // 2
    out_partner[...] = (dot_nn(mixed[1, x], own[...]) + dot_nn(mixed[1, 1 - x], other[...])).astype(bf16)


def project_back_body(
    pair, middle, further, seg_col, feat_k, values, dk_intra, dv_intra, d_query,
    q0, q1, q2, q3, w0, w1, w2, w3, w3_other, own, partner, work,
):
    q = (q0[...], q1[: w0.shape[0], PAIR_Q], q2[...], q3[...])
    w = (w0[...], w1[: w0.shape[0], KV_COLUMNS], w2[...])
    for i in (1, 0):
        ids, total = received(-1, pair, middle, further, i)
        take = seg_col[i] == ids
        d_key, d_value = [], []
        for g in range(2):
            back = total[head(g)]
            k, v = feat_k[i, g], values[i, g]
            dk = dk_intra[i, g] + jnp.where(take, dot_nt(v, back), 0.0)
            dv = dv_intra[i, g] + jnp.where(take, dot_nn(k, back), 0.0)
            d_key.append((dk * jnp.minimum(k.astype(f32), 1.0)).astype(bf16))
            d_value.append(dv.astype(bf16))
        d_proj = jnp.concatenate(d_key + d_value, axis=1)
        pieces = [(j, slice(None), dot_nt(d_proj, w[j])) for j in range(3)]
        pieces += [
            (3, columns(at, part.shape[0]), dot_nt(d_proj, part[...])) for at, part in zip(halves(), (w3, w3_other))
        ]
        for j in range(4):
            from_q = dot_nt(d_query[i], q[j])
            if i == 1:
                work[j ^ 1] = from_q
            else:
                own[j] = from_q
        for j, at, value in pieces:
            if i == 1:
                partner[j ^ 1, :, at] = (work[j ^ 1, :, at] + value).astype(bf16)
            else:
                own[j, :, at] += value


def final_body(
    own, partner, out_partner, tokens, cot, inv_rms, gain, mixed, w_own, w_other, output, grad, work
):
    x = lax.axis_index("dp") // 2
    total = dot_nn(mixed[0, x], w_own[...]) + dot_nn(mixed[0, 1 - x], w_other[...])
    output[...] = (tokens[...].astype(f32) + (total + out_partner[...].astype(f32))).astype(bf16)
    inner = None
    for j in range(4):
        at = columns(lax.axis_index("dp") ^ j, 256)
        norm_grad = (own[j] + partner[j].astype(f32)) * gain[:, at]
        work[j] = norm_grad
        part = jnp.sum(tokens[:, at].astype(f32) * norm_grad, axis=1, keepdims=True)
        inner = part if inner is None else inner + part
    inv = inv_rms[...]
    scale = inv**3 * (inner * (1.0 / D))
    for j in range(4):
        at = columns(lax.axis_index("dp") ^ j, 256)
        value = cot[:, at].astype(f32) + inv * work[j] - tokens[:, at].astype(f32) * scale
        grad[:, at] = value.astype(bf16)


def flip(array, axis, bit):
    n = lax.axis_size(axis)
    return lax.ppermute(array, axis, [(i, i ^ bit) for i in range(n)])


def shift(array, axis, step):
    n = lax.axis_size(axis)
    return lax.ppermute(array, axis, [(i, i + step) for i in range(n) if 0 <= i + step < n])


def carry(message, middle, further, ends, step, late=None):
    n = lax.axis_size("seq")
    if n == 4:
        middle = lax.ppermute(middle, "seq", [(1, 2), (2, 1)])
        return flip(message if late is None else late, "seq", 1), middle, flip(further, "seq", 2)
    position = lax.axis_index("seq")
    begin, end = (ends[0], ends[1]) if step > 0 else (ends[1], ends[0])
    total = message[:, : 2 * HEAD_DIM].astype(f32)
    reach = 1
    while reach < n:
        before = shift(total, "seq", step * reach)
        ids = shift(jnp.stack([begin, end]), "seq", step * reach)
        there = position - step * reach
        there = (there >= 0) & (there < n)
        goes_on = there & (begin == end) & (ids[1] == begin)
        total = total + jnp.where(goes_on[:, None, None], before, 0.0)
        begin = jnp.where(there, ids[0], begin)
        reach *= 2
    rows = jnp.concatenate([total.astype(bf16), message[:, 2 * HEAD_DIM :]], axis=1)
    near = shift(rows, "seq", step)
    return near, near, near


def reduce_weight(rest, a_send, b_send, back, ends, d_attn):
    n = lax.axis_size("seq")
    half, width = a_send.shape
    quarter = half // 2
    kept, a_send, b_send = call(
        weight_one_body,
        [((half, width), f32), ((quarter, width), bf16), ((quarter, width), bf16)],
        rest, flip(a_send, "dp", 2), flip(b_send, "seq", 1), us=W1,
    )
    a_send, back_late = lax.optimization_barrier((a_send, back[0]))
    back_near = carry(*back, ends, -1, back_late)
    outs = [((half, width), f32), ((half, width), bf16)]
    kept, send = call(weight_two_body, outs, kept, flip(a_send, "seq", 1), flip(b_send, "dp", 2), us=W2)
    send, d_attn = lax.optimization_barrier((send, d_attn))
    reach = 2
    while reach < n:
        kept, send = call(weight_three_body, outs, kept, flip(send, "seq", reach), us=W3)
        reach *= 2
    return kept, send, back_near, d_attn


def shards(tokens, segment_ids, norm_gain, w_qkv, head_gain, w_out, cotangent):
    length = segment_ids.shape[1]
    width = HEADS * HEAD_DIM
    n = lax.axis_size("seq")
    flat = tokens.reshape(length, D)
    cot = cotangent.reshape(length, D)
    gain = norm_gain.reshape(1, D)
    gain_h = head_gain.reshape(1, width)
    wide = (2, 2, length, HEAD_DIM)

    shard_rows = w_qkv.shape[0]
    (kv_half,) = split(split_half_body, [(shard_rows // 2, 4 * HEAD_DIM)], 4, 1.0, w_qkv)
    kv_diagonal = flip(kv_half, "dp", 3)
    kv_mine, kv_other = split(
        split_kv_body,
        [(shard_rows, 4 * HEAD_DIM), (shard_rows + ID_ROWS, 6 * HEAD_DIM)],
        10, SPLIT, w_qkv, segment_ids, kv_half, specs=(VMEM, ANY),
    )
    kv_half, flat, cot = lax.optimization_barrier((kv_half, flat, cot))
    kv_x, kv_pair = flip(kv_mine, "dp", 2), flip(kv_other, "dp", 1)
    partner, cot_partner = flip(flat, "dp", 1), flip(cot, "dp", 1)
    kv_diagonal_other = flip(kv_diagonal, "groups", 1)
    kv_diagonal, partner, cot_partner, w_late = lax.optimization_barrier((kv_diagonal, partner, cot_partner, w_qkv))
    normed, inv_rms, raw_near = call(
        prep_body,
        [((4, 2 * length, D // 4), bf16), ((length, 1), f32), ((2 * length, 4 * HEAD_DIM), f32)],
        flat, partner, gain, kv_mine, us=PREP,
    )
    q_mine, q_other = split(split_q_body, [(shard_rows, 2 * HEAD_DIM)] * 2, 4, 1.0, w_late)
    inv_rms, q_mine, q_other, out_own, kv_pair = lax.optimization_barrier((inv_rms, q_mine, q_other, w_out, kv_pair))
    wq = [q_mine, kv_pair, flip(q_mine, "dp", 2), flip(q_other, "dp", 3)]
    kv = [kv_mine, kv_pair, kv_x, kv_diagonal, kv_diagonal_other]
    out = [out_own, flip(out_own, "dp", 2)]

    messages = [((2, 2 * HEAD_DIM + m * ID_ROWS, HEAD_DIM), bf16) for m in (1, 1, 2)]
    feat_k, values, state, state_mid, state_far, seg_col, seg_row = call(
        kv_body,
        [(wide, bf16), (wide, bf16), *messages, ((2, length, HEAD_DIM), f32), ((2, 1, length), f32)],
        raw_near, normed, segment_ids, *kv[1:],
    )
    ends = jnp.stack([seg_col[:, 0, 0], seg_col[:, -1, 0]])
    near = carry(state, state_mid, state_far, ends, 1)
    feat_q, intra = call(
        query_body, [(wide, bf16), (wide, f32)], normed, *wq, feat_k, values, seg_col, seg_row, us=QUERY
    )
    feat_q, cot_late = lax.optimization_barrier((feat_q, cot_partner))
    (upstream,) = call(
        mixed_grad_body, [(wide, f32)], cot, cot_late, *out, gain_h, us=MIXED
    )
    rows = HEAD_DIM // 2
    mixed, d_attn, back, back_mid, back_far, before, rest, a_send, b_send = call(
        attn_body,
        [
            (wide, bf16),
            (wide, bf16),
            *messages,
            ((2, 2 * HEAD_DIM, HEAD_DIM), bf16),
            ((2 * rows, D), f32),
            ((rows, D), bf16),
            ((2, rows // 2, D), bf16),
        ],
        *near, seg_col, feat_q, intra, upstream, gain_h, cot, cot_partner,
    )
    scale = 1.0 / math.sqrt(length * lax.axis_size("dp") * n)
    kept, sent, back_near, d_attn = reduce_weight(rest, a_send, b_send, (back, back_mid, back_far), ends, d_attn)
    (out_partner,) = call(partner_output_body, [((length, D), bf16)], mixed, *out, us=FILL)
    d_query, dk_intra, dv_intra = call(
        back_body,
        [((2, length, 2 * HEAD_DIM), bf16), (wide, f32), (wide, f32)],
        near[0], before, near[1], seg_col, seg_row, d_attn, values, feat_k, feat_q, us=BACK,
    )
    own, theirs = call(
        project_back_body,
        [((4, length, D // 4), f32), ((4, length, D // 4), bf16)],
        *back_near, seg_col, feat_k, values, dk_intra, dv_intra, d_query,
        *wq, *kv, us=PROJECT, scratch=[((4, length, D // 4), f32)],
    )
    theirs, out_partner = lax.optimization_barrier((theirs, out_partner))
    output, grad = call(
        final_body,
        [((length, D), bf16), ((length, D), bf16)],
        own, flip(theirs, "dp", 1), flip(out_partner, "dp", 1), flat, cot, inv_rms, gain, mixed, *out,
        scratch=[((4, length, D // 4), f32)],
    )
    arrived = flip(sent, "seq", 1)
    output, grad, kept = lax.optimization_barrier((output, grad, kept))
    (grad_out_weight,) = call(
        functools.partial(weight_last_body, scale), [((HEAD_DIM, D), f32)], kept, arrived
    )
    return (output.reshape(tokens.shape), grad.reshape(tokens.shape), grad_out_weight)


def solution(mesh):
    in_specs = (
        P(("groups", "dp"), "seq", None),
        P(("groups", "dp"), "seq"),
        P(),
        P("dp", None),
        P(),
        P("dp", None),
        P(("groups", "dp"), "seq", None),
    )
    out_specs = (
        P(("groups", "dp"), "seq", None),
        P(("groups", "dp"), "seq", None),
        P(("groups", "dp"), None),
    )
    return jax.shard_map(shards, mesh=mesh, in_specs=in_specs, out_specs=out_specs, check_vma=False)
```

```python
import functools
import math

import jax
import jax.numpy as jnp
from jax import lax
from jax.experimental import pallas as pl
from jax.experimental.pallas import tpu as pltpu
from jax.sharding import PartitionSpec as P

D = 1024
HEADS = 4
HEAD_DIM = 128
ID_ROWS = 16

epsilon = 1e-06
W1, W2, W3, PREP, QUERY, MIXED, BACK, PROJECT, SPLIT, FILL = 8.0, 8.0, 8.0, 20.0, 0.5, 0.1, 0.1, 2.0, 20.0, 2.0

f32 = jnp.float32
bf16 = jnp.bfloat16


def dot_nn(a, b):
    return lax.dot_general(a, b, (((1,), (0,)), ((), ())), preferred_element_type=f32)


def dot_nt(a, b):
    return lax.dot_general(a, b, (((1,), (1,)), ((), ())), preferred_element_type=f32)


def dot_tn(a, b):
    return lax.dot_general(a, b, (((0,), (0,)), ((), ())), preferred_element_type=f32)


def feature_map(u):
    return jnp.where(u > 0, u + 1.0, jnp.exp(jnp.minimum(u, 0.0)))


def head(h):
    return slice(h * HEAD_DIM, (h + 1) * HEAD_DIM)


VMEM = pl.BlockSpec(memory_space=pltpu.VMEM)
ANY = pl.BlockSpec(memory_space=pl.ANY)


def call(body, outs, *args, scratch=(), us=2.0):
    return pl.pallas_call(
        body,
        out_shape=[jax.ShapeDtypeStruct(shape, dtype) for shape, dtype in outs],
        in_specs=[VMEM] * len(args),
        out_specs=[VMEM] * len(outs),
        scratch_shapes=[pltpu.VMEM(shape, dtype) for shape, dtype in scratch],
        compiler_params=pltpu.CompilerParams(vmem_limit_bytes=16 * 1024 * 1024),
        cost_estimate=pl.CostEstimate(flops=int(us * 1e9), transcendentals=0, bytes_accessed=int(us * 3e6)),
    )(*args)


def columns(index, width):
    return pl.ds(pl.multiple_of(index * width, width), width)


def causal(seg_col, seg_row, i):
    length = seg_row.shape[2]
    order = lax.broadcasted_iota(jnp.int32, (length, length), 0) >= lax.broadcasted_iota(
        jnp.int32, (length, length), 1
    )
    down = jnp.concatenate([seg_col[i]] * (length // HEAD_DIM), axis=1)
    return (down == seg_row[i]) & order


def run_all(copies, sem):
    copies = [pltpu.make_async_copy(source, target, sem.at[n]) for n, (source, target) in enumerate(copies)]
    for copy in copies:
        copy.start()
    for copy in copies:
        copy.wait()


def kv_columns(n, which):
    return columns(4 + 4 * (n // 2) + 2 * (n % 2) + which, HEAD_DIM)


def split_half_body(w, half, sem):
    c, rows = lax.axis_index("dp") % 2, half.shape[0]
    part = pl.ds(pl.multiple_of(lax.axis_index("groups") * rows, rows), rows)
    run_all([(w.at[part, kv_columns(n, 1 - c)], half.at[:, head(n)]) for n in range(4)], sem)


def split_kv_body(w, seg, _, mine, other, sem):
    c = lax.axis_index("dp") % 2
    rows, length = w.shape[0], seg.shape[1]
    other[rows:, :length] = jnp.broadcast_to(seg[...].astype(f32), (ID_ROWS, length)).astype(bf16)
    copies = []
    for target, which in ((mine, c), (other, 1 - c)):
        copies += [(w.at[:, kv_columns(n, which)], target.at[:rows, head(n)]) for n in range(4)]
    copies += [(w.at[:, columns(2 * g + 1 - c, HEAD_DIM)], other.at[:rows, head(4 + g)]) for g in range(2)]
    run_all(copies, sem)


def split_q_body(w, mine, other, sem):
    c = lax.axis_index("dp") % 2
    copies = []
    for target, which in ((mine, c), (other, 1 - c)):
        copies += [(w.at[:, columns(2 * g + which, HEAD_DIM)], target.at[:, head(g)]) for g in range(2)]
    run_all(copies, sem)


def split(body, shapes, copies, us, w, *rest, specs=()):
    return pl.pallas_call(
        body,
        out_shape=[jax.ShapeDtypeStruct(shape, bf16) for shape in shapes],
        in_specs=[ANY, *specs],
        out_specs=[VMEM] * len(shapes),
        scratch_shapes=[pltpu.SemaphoreType.DMA((copies,))],
        compiler_params=pltpu.CompilerParams(vmem_limit_bytes=8 * 1024 * 1024),
        cost_estimate=pl.CostEstimate(flops=int(us * 1e9), transcendentals=0, bytes_accessed=10**6),
    )(w, *rest)


KV_COLUMNS = slice(0, 4 * HEAD_DIM)
PAIR_Q = slice(4 * HEAD_DIM, 6 * HEAD_DIM)


def halves():
    at = lax.axis_index("groups")
    return at, 1 - at


def sources(step):
    at, n = lax.axis_index("seq"), lax.axis_size("seq")
    if n != 4:
        return at < 0, at < 0
    return (at % 2 == 1, at >= 2) if step > 0 else (at % 2 == 0, at < 2)


def pair_body(near, normed, seg, w1, raw, seg_col, seg_row):
    rows, length = w1.shape[0] - ID_ROWS, seg.shape[1]
    for i, ids in enumerate((seg[...].astype(f32), w1[rows : rows + 1, :length].astype(f32))):
        seg_row[i] = ids
        seg_col[i] = jnp.broadcast_to(ids, (HEAD_DIM, length)).T
    raw[...] = near[...] + dot_nn(normed[1], w1[:rows, KV_COLUMNS])


def prep_body(tokens, partner, gain, w0, normed, inv_rms, raw):
    length = tokens.shape[0]
    for i, part in enumerate((tokens, partner)):
        x = part[...].astype(f32)
        inv = lax.rsqrt(jnp.mean(x * x, axis=1, keepdims=True) + epsilon)
        if i == 0:
            inv_rms[...] = inv
        for j in range(4):
            at = columns(lax.axis_index("dp") ^ j, 256)
            normed[j, i * length : (i + 1) * length] = (part[:, at].astype(f32) * inv * gain[:, at]).astype(bf16)
    raw[...] = dot_nn(normed[0], w0[...])


def store_state(targets, i, g, value):
    for target in targets:
        target[i, head(g), :] = value.astype(bf16)


def store_ids(targets, i, ids):
    for target in targets:
        rows = target.shape[1] - 2 * HEAD_DIM
        target[i, 2 * HEAD_DIM :, :] = jnp.broadcast_to(ids, (rows, HEAD_DIM)).astype(bf16)


def kv_body(near, normed, w2, w3, w3_other, seg_col, feat_k, values, state, state_mid, state_far):
    length = seg_col.shape[1]
    raw = near[...] + dot_nn(normed[2], w2[...])
    for at, w in zip(halves(), (w3, w3_other)):
        raw += dot_nn(normed[3, :, columns(at, w.shape[0])], w[...])
    raw = raw.astype(bf16)
    for i in range(2):
        last = seg_col[i, length - 1 : length, :]
        tail = seg_col[i] == last
        rows = slice(i * length, (i + 1) * length)
        for g in range(2):
            k = feature_map(raw[rows, head(g)].astype(f32))
            v = raw[rows, head(2 + g)]
            feat_k[i, g] = k.astype(bf16)
            values[i, g] = v
            store_state((state, state_mid, state_far), i, g, dot_tn(jnp.where(tail, k, 0.0).astype(bf16), v))
        store_ids((state, state_mid, state_far), i, last)


def query_body(normed, w0, w1, w2, w3, feat_k, values, seg_col, seg_row, feat_q, intra):
    raw = dot_nn(normed[0], w0[...]) + dot_nn(normed[1], w1[: w0.shape[0], PAIR_Q])
    raw += dot_nn(normed[2], w2[...]) + dot_nn(normed[3], w3[...])
    raw = raw.astype(bf16)
    length = seg_row.shape[2]
    for i in range(2):
        mask = causal(seg_col, seg_row, i)
        for g in range(2):
            q = feature_map(raw[i * length : (i + 1) * length, head(g)].astype(f32)).astype(bf16)
            feat_q[i, g] = q
            s = jnp.where(mask, dot_nt(q, feat_k[i, g]), 0.0).astype(bf16)
            intra[i, g] = dot_nn(s, values[i, g])


def mixed_grad_body(cot, cot_partner, own, other, gain, upstream):
    for j, o in enumerate((own, other)):
        full = lax.axis_index("dp") ^ (2 * j)
        for i, part in enumerate((cot, cot_partner)):
            upstream[i, full // 2] = dot_nt(part[...], o[...]) * gain[:, columns(full, HEAD_DIM)]


def received(step, pair, middle, further, i):
    use_pair, use_further = sources(step)
    used = 2 * HEAD_DIM + ID_ROWS
    near = jnp.where(use_pair, pair[i, :used].astype(f32), middle[i, :used].astype(f32))
    ids = near[2 * HEAD_DIM : 2 * HEAD_DIM + 1, :]
    far = further[i, :used].astype(f32)
    same = (far[2 * HEAD_DIM : 2 * HEAD_DIM + 1, :] == ids) & use_further
    total = near[: 2 * HEAD_DIM] + jnp.where(same, far[: 2 * HEAD_DIM], 0.0)
    return ids, total.astype(bf16)


def attn_body(
    pair, middle, further, seg_col, feat_q, intra, upstream, gain, cot, cot_partner,
    mixed, d_attn, state, state_mid, state_far, before, rest, a_send, b_send,
):
    for i in range(2):
        first = seg_col[i, 0:1, :]
        begin = seg_col[i] == first
        ids, total = received(1, pair, middle, further, i)
        before[i] = total
        take = seg_col[i] == ids
        for g in range(2):
            q = feat_q[i, g]
            attention = intra[i, g] + jnp.where(take, dot_nn(q, total[head(g)]), 0.0)
            ratio = lax.rsqrt(jnp.mean(attention * attention, axis=1, keepdims=True) + epsilon)
            mixed[i, g] = (attention * ratio * gain[:, columns(2 * g + lax.axis_index("dp") % 2, HEAD_DIM)]).astype(bf16)
            up = upstream[i, g]
            inner = jnp.mean(attention * up, axis=1, keepdims=True)
            da = (ratio * up - ratio**3 * attention * inner).astype(bf16)
            d_attn[i, g] = da
            store_state((state, state_mid, state_far), i, g, dot_tn(jnp.where(begin, q.astype(f32), 0.0).astype(bf16), da))
        store_ids((state, state_mid, state_far), i, first)
    half = HEAD_DIM // 2
    quarter = half // 2
    second = lax.axis_index("seq") % 2 == 1
    for j in range(2):
        g = (lax.axis_index("dp") ^ (2 * j)) // 2
        part = dot_tn(mixed[0, g], cot[...]) + dot_tn(mixed[1, g], cot_partner[...])
        if j == 0:
            rest[:half] = part[:half]
        else:
            a_send[...] = part[:half].astype(bf16)
        low, high = part[half : half + quarter], part[half + quarter :]
        rest[half + j * quarter : half + (j + 1) * quarter] = jnp.where(second, high, low)
        b_send[j] = jnp.where(second, low, high).astype(bf16)


def weight_one_body(rest, a_in, b_in, kept, a_send, b_send):
    second = lax.axis_index("seq") % 2 == 1
    quarter = b_in.shape[1]
    low = rest[:quarter] + a_in[:quarter].astype(f32)
    high = rest[quarter : 2 * quarter] + a_in[quarter:].astype(f32)
    kept[:quarter] = jnp.where(second, high, low)
    a_send[...] = jnp.where(second, low, high).astype(bf16)
    kept[quarter:] = rest[2 * quarter : 3 * quarter] + b_in[0].astype(f32)
    b_send[...] = (rest[3 * quarter :] + b_in[1].astype(f32)).astype(bf16)


def weight_two_body(kept, a_in, b_in, total, send):
    quarter = a_in.shape[0]
    total[:quarter] = kept[:quarter] + a_in[...].astype(f32)
    total[quarter:] = kept[quarter:] + b_in[...].astype(f32)
    send[...] = total[...].astype(bf16)


def weight_three_body(kept, arrived, total, send):
    total[...] = kept[...] + arrived[...].astype(f32)
    send[...] = total[...].astype(bf16)


def weight_last_body(scale, kept, arrived, grad):
    quarter = kept.shape[0] // 2
    second = lax.axis_index("seq") % 2 == 1
    mine, theirs = kept[...] * scale, arrived[...].astype(f32) * scale
    low = jnp.where(second, theirs, mine)
    high = jnp.where(second, mine, theirs)
    for n, part in enumerate((low[:quarter], high[:quarter], low[quarter:], high[quarter:])):
        grad[n * quarter : (n + 1) * quarter] = part


def back_body(
    pair, before, middle, seg_col, seg_row, d_attn, values, feat_k, feat_q,
    d_query, dk_intra, dv_intra,
):
    for i in range(2):
        mask = causal(seg_col, seg_row, i)
        use_pair, _ = sources(1)
        last = 2 * HEAD_DIM
        ids = jnp.where(use_pair, pair[i, last : last + 1].astype(f32), middle[i, last : last + 1].astype(f32))
        take = seg_col[i] == ids
        for g in range(2):
            da, q, k = d_attn[i, g], feat_q[i, g], feat_k[i, g]
            s = jnp.where(mask, dot_nt(q, k), 0.0).astype(bf16)
            ds = jnp.where(mask, dot_nt(da, values[i, g]), 0.0).astype(bf16)
            dq = dot_nn(ds, k) + jnp.where(take, dot_nt(da, before[i, head(g)]), 0.0)
            d_query[i, :, head(g)] = (dq * jnp.minimum(q.astype(f32), 1.0)).astype(bf16)
            dk_intra[i, g] = dot_tn(ds, q)
            dv_intra[i, g] = dot_tn(s, da)


def partner_output_body(mixed, own, other, out_partner):
    x = lax.axis_index("dp") // 2
    out_partner[...] = (dot_nn(mixed[1, x], own[...]) + dot_nn(mixed[1, 1 - x], other[...])).astype(bf16)


def project_back_body(
    pair, middle, further, seg_col, feat_k, values, dk_intra, dv_intra, d_query,
    q0, q1, q2, q3, w0, w1, w2, w3, w3_other, own, partner, work,
):
    q = (q0[...], q1[: w0.shape[0], PAIR_Q], q2[...], q3[...])
    w = (w0[...], w1[: w0.shape[0], KV_COLUMNS], w2[...])
    for i in (1, 0):
        ids, total = received(-1, pair, middle, further, i)
        take = seg_col[i] == ids
        d_key, d_value = [], []
        for g in range(2):
            back = total[head(g)]
            k, v = feat_k[i, g], values[i, g]
            dk = dk_intra[i, g] + jnp.where(take, dot_nt(v, back), 0.0)
            dv = dv_intra[i, g] + jnp.where(take, dot_nn(k, back), 0.0)
            d_key.append((dk * jnp.minimum(k.astype(f32), 1.0)).astype(bf16))
            d_value.append(dv.astype(bf16))
        d_proj = jnp.concatenate(d_key + d_value, axis=1)
        pieces = [(j, slice(None), dot_nt(d_proj, w[j])) for j in range(3)]
        pieces += [
            (3, columns(at, part.shape[0]), dot_nt(d_proj, part[...])) for at, part in zip(halves(), (w3, w3_other))
        ]
        for j in range(4):
            from_q = dot_nt(d_query[i], q[j])
            if i == 1:
                work[j ^ 1] = from_q
            else:
                own[j] = from_q
        for j, at, value in pieces:
            if i == 1:
                partner[j ^ 1, :, at] = (work[j ^ 1, :, at] + value).astype(bf16)
            else:
                own[j, :, at] += value


def final_body(
    own, partner, out_partner, tokens, cot, inv_rms, gain, mixed, w_own, w_other, output, grad, work
):
    x = lax.axis_index("dp") // 2
    total = dot_nn(mixed[0, x], w_own[...]) + dot_nn(mixed[0, 1 - x], w_other[...])
    output[...] = (tokens[...].astype(f32) + (total + out_partner[...].astype(f32))).astype(bf16)
    inner = None
    for j in range(4):
        at = columns(lax.axis_index("dp") ^ j, 256)
        norm_grad = (own[j] + partner[j].astype(f32)) * gain[:, at]
        work[j] = norm_grad
        part = jnp.sum(tokens[:, at].astype(f32) * norm_grad, axis=1, keepdims=True)
        inner = part if inner is None else inner + part
    inv = inv_rms[...]
    scale = inv**3 * (inner * (1.0 / D))
    for j in range(4):
        at = columns(lax.axis_index("dp") ^ j, 256)
        value = cot[:, at].astype(f32) + inv * work[j] - tokens[:, at].astype(f32) * scale
        grad[:, at] = value.astype(bf16)


def flip(array, axis, bit):
    n = lax.axis_size(axis)
    return lax.ppermute(array, axis, [(i, i ^ bit) for i in range(n)])


def shift(array, axis, step):
    n = lax.axis_size(axis)
    return lax.ppermute(array, axis, [(i, i + step) for i in range(n) if 0 <= i + step < n])


def carry(message, middle, further, ends, step, late=None):
    n = lax.axis_size("seq")
    if n == 4:
        middle = lax.ppermute(middle, "seq", [(1, 2), (2, 1)])
        return flip(message if late is None else late, "seq", 1), middle, flip(further, "seq", 2)
    position = lax.axis_index("seq")
    begin, end = (ends[0], ends[1]) if step > 0 else (ends[1], ends[0])
    total = message[:, : 2 * HEAD_DIM].astype(f32)
    reach = 1
    while reach < n:
        before = shift(total, "seq", step * reach)
        ids = shift(jnp.stack([begin, end]), "seq", step * reach)
        there = position - step * reach
        there = (there >= 0) & (there < n)
        goes_on = there & (begin == end) & (ids[1] == begin)
        total = total + jnp.where(goes_on[:, None, None], before, 0.0)
        begin = jnp.where(there, ids[0], begin)
        reach *= 2
    rows = jnp.concatenate([total.astype(bf16), message[:, 2 * HEAD_DIM :]], axis=1)
    near = shift(rows, "seq", step)
    return near, near, near


def reduce_weight(rest, a_send, b_send, back, ends, d_attn):
    n = lax.axis_size("seq")
    half, width = a_send.shape
    quarter = half // 2
    kept, a_send, b_send = call(
        weight_one_body,
        [((half, width), f32), ((quarter, width), bf16), ((quarter, width), bf16)],
        rest, flip(a_send, "dp", 2), flip(b_send, "seq", 1), us=W1,
    )
    a_send, back_late = lax.optimization_barrier((a_send, back[0]))
    back_near = carry(*back, ends, -1, back_late)
    outs = [((half, width), f32), ((half, width), bf16)]
    kept, send = call(weight_two_body, outs, kept, flip(a_send, "seq", 1), flip(b_send, "dp", 2), us=W2)
    send, d_attn = lax.optimization_barrier((send, d_attn))
    reach = 2
    while reach < n:
        kept, send = call(weight_three_body, outs, kept, flip(send, "seq", reach), us=W3)
        reach *= 2
    return kept, send, back_near, d_attn


def shards(tokens, segment_ids, norm_gain, w_qkv, head_gain, w_out, cotangent):
    length = segment_ids.shape[1]
    width = HEADS * HEAD_DIM
    n = lax.axis_size("seq")
    flat = tokens.reshape(length, D)
    cot = cotangent.reshape(length, D)
    gain = norm_gain.reshape(1, D)
    gain_h = head_gain.reshape(1, width)
    wide = (2, 2, length, HEAD_DIM)

    shard_rows = w_qkv.shape[0]
    w_first = pltpu.with_memory_space_constraint(w_qkv, pltpu.HBM)
    (kv_half,) = split(split_half_body, [(shard_rows // 2, 4 * HEAD_DIM)], 4, 1.0, w_first)
    kv_diagonal = flip(kv_half, "dp", 3)
    kv_mine, kv_other = split(
        split_kv_body,
        [(shard_rows, 4 * HEAD_DIM), (shard_rows + ID_ROWS, 6 * HEAD_DIM)],
        10, SPLIT, w_qkv, segment_ids, kv_half, specs=(VMEM, ANY),
    )
    kv_half, flat, cot = lax.optimization_barrier((kv_half, flat, cot))
    kv_x, kv_pair = flip(kv_mine, "dp", 2), flip(kv_other, "dp", 1)
    partner, cot_partner = flip(flat, "dp", 1), flip(cot, "dp", 1)
    kv_diagonal_other = flip(kv_diagonal, "groups", 1)
    kv_diagonal, partner, cot_partner, w_late = lax.optimization_barrier((kv_diagonal, partner, cot_partner, w_qkv))
    normed, inv_rms, raw_near = call(
        prep_body,
        [((4, 2 * length, D // 4), bf16), ((length, 1), f32), ((2 * length, 4 * HEAD_DIM), f32)],
        flat, partner, gain, kv_mine, us=PREP,
    )
    raw_near, seg_col, seg_row = call(
        pair_body,
        [((2 * length, 4 * HEAD_DIM), f32), ((2, length, HEAD_DIM), f32), ((2, 1, length), f32)],
        raw_near, normed, segment_ids, kv_pair,
    )
    q_mine, q_other = split(split_q_body, [(shard_rows, 2 * HEAD_DIM)] * 2, 4, 1.0, w_late)
    raw_near, q_mine, q_other, out_own = lax.optimization_barrier((raw_near, q_mine, q_other, w_out))
    wq = [q_mine, kv_pair, flip(q_mine, "dp", 2), flip(q_other, "dp", 3)]
    kv = [kv_mine, kv_pair, kv_x, kv_diagonal, kv_diagonal_other]
    out = [out_own, flip(out_own, "dp", 2)]

    messages = [((2, 2 * HEAD_DIM + m * ID_ROWS, HEAD_DIM), bf16) for m in (1, 1, 2)]
    feat_k, values, state, state_mid, state_far = call(
        kv_body, [(wide, bf16), (wide, bf16), *messages], raw_near, normed, *kv[2:], seg_col
    )
    ends = jnp.stack([seg_col[:, 0, 0], seg_col[:, -1, 0]])
    near = carry(state, state_mid, state_far, ends, 1)
    feat_q, intra = call(
        query_body, [(wide, bf16), (wide, f32)], normed, *wq, feat_k, values, seg_col, seg_row, us=QUERY
    )
    feat_q, cot_late = lax.optimization_barrier((feat_q, cot_partner))
    (upstream,) = call(
        mixed_grad_body, [(wide, f32)], cot, cot_late, *out, gain_h, us=MIXED
    )
    rows = HEAD_DIM // 2
    mixed, d_attn, back, back_mid, back_far, before, rest, a_send, b_send = call(
        attn_body,
        [
            (wide, bf16),
            (wide, bf16),
            *messages,
            ((2, 2 * HEAD_DIM, HEAD_DIM), bf16),
            ((2 * rows, D), f32),
            ((rows, D), bf16),
            ((2, rows // 2, D), bf16),
        ],
        *near, seg_col, feat_q, intra, upstream, gain_h, cot, cot_partner,
    )
    scale = 1.0 / math.sqrt(length * lax.axis_size("dp") * n)
    kept, sent, back_near, d_attn = reduce_weight(rest, a_send, b_send, (back, back_mid, back_far), ends, d_attn)
    (out_partner,) = call(partner_output_body, [((length, D), bf16)], mixed, *out, us=FILL)
    d_query, dk_intra, dv_intra = call(
        back_body,
        [((2, length, 2 * HEAD_DIM), bf16), (wide, f32), (wide, f32)],
        near[0], before, near[1], seg_col, seg_row, d_attn, values, feat_k, feat_q, us=BACK,
    )
    own, theirs = call(
        project_back_body,
        [((4, length, D // 4), f32), ((4, length, D // 4), bf16)],
        *back_near, seg_col, feat_k, values, dk_intra, dv_intra, d_query,
        *wq, *kv, us=PROJECT, scratch=[((4, length, D // 4), f32)],
    )
    theirs, out_partner = lax.optimization_barrier((theirs, out_partner))
    output, grad = call(
        final_body,
        [((length, D), bf16), ((length, D), bf16)],
        own, flip(theirs, "dp", 1), flip(out_partner, "dp", 1), flat, cot, inv_rms, gain, mixed, *out,
        scratch=[((4, length, D // 4), f32)],
    )
    arrived = flip(sent, "seq", 1)
    output, grad, kept = lax.optimization_barrier((output, grad, kept))
    (grad_out_weight,) = call(
        functools.partial(weight_last_body, scale), [((HEAD_DIM, D), f32)], kept, arrived
    )
    return (output.reshape(tokens.shape), grad.reshape(tokens.shape), grad_out_weight)


def solution(mesh):
    in_specs = (
        P(("groups", "dp"), "seq", None),
        P(("groups", "dp"), "seq"),
        P(),
        P("dp", None),
        P(),
        P("dp", None),
        P(("groups", "dp"), "seq", None),
    )
    out_specs = (
        P(("groups", "dp"), "seq", None),
        P(("groups", "dp"), "seq", None),
        P(("groups", "dp"), None),
    )
    return jax.shard_map(shards, mesh=mesh, in_specs=in_specs, out_specs=out_specs, check_vma=False)
```

```python
import functools
import math

import jax
import jax.numpy as jnp
from jax import lax
from jax.experimental import pallas as pl
from jax.experimental.pallas import tpu as pltpu
from jax.sharding import PartitionSpec as P

D = 1024
HEADS = 4
HEAD_DIM = 128
ID_ROWS = 16

epsilon = 1e-06
W1, W2, W3, PREP, QUERY, MIXED, BACK, PROJECT, SPLIT, FILL = 8.0, 8.0, 8.0, 20.0, 0.5, 0.1, 0.1, 2.0, 20.0, 2.0

f32 = jnp.float32
bf16 = jnp.bfloat16


def dot_nn(a, b):
    return lax.dot_general(a, b, (((1,), (0,)), ((), ())), preferred_element_type=f32)


def dot_nt(a, b):
    return lax.dot_general(a, b, (((1,), (1,)), ((), ())), preferred_element_type=f32)


def dot_tn(a, b):
    return lax.dot_general(a, b, (((0,), (0,)), ((), ())), preferred_element_type=f32)


def feature_map(u):
    return jnp.where(u > 0, u + 1.0, jnp.exp(jnp.minimum(u, 0.0)))


def head(h):
    return slice(h * HEAD_DIM, (h + 1) * HEAD_DIM)


VMEM = pl.BlockSpec(memory_space=pltpu.VMEM)
ANY = pl.BlockSpec(memory_space=pl.ANY)


def call(body, outs, *args, scratch=(), us=2.0):
    return pl.pallas_call(
        body,
        out_shape=[jax.ShapeDtypeStruct(shape, dtype) for shape, dtype in outs],
        in_specs=[VMEM] * len(args),
        out_specs=[VMEM] * len(outs),
        scratch_shapes=[pltpu.VMEM(shape, dtype) for shape, dtype in scratch],
        compiler_params=pltpu.CompilerParams(vmem_limit_bytes=16 * 1024 * 1024),
        cost_estimate=pl.CostEstimate(flops=int(us * 1e9), transcendentals=0, bytes_accessed=int(us * 3e6)),
    )(*args)


def columns(index, width):
    return pl.ds(pl.multiple_of(index * width, width), width)


def causal(seg_col, seg_row, i):
    length = seg_row.shape[2]
    order = lax.broadcasted_iota(jnp.int32, (length, length), 0) >= lax.broadcasted_iota(
        jnp.int32, (length, length), 1
    )
    down = jnp.concatenate([seg_col[i]] * (length // HEAD_DIM), axis=1)
    return (down == seg_row[i]) & order


def run_all(copies, sem):
    copies = [pltpu.make_async_copy(source, target, sem.at[n]) for n, (source, target) in enumerate(copies)]
    for copy in copies:
        copy.start()
    for copy in copies:
        copy.wait()


def kv_columns(n, which):
    return columns(4 + 4 * (n // 2) + 2 * (n % 2) + which, HEAD_DIM)


def split_half_body(w, half, sem):
    c, rows = lax.axis_index("dp") % 2, half.shape[0]
    part = pl.ds(pl.multiple_of(lax.axis_index("groups") * rows, rows), rows)
    run_all([(w.at[part, kv_columns(n, 1 - c)], half.at[:, head(n)]) for n in range(4)], sem)


def split_kv_body(w, seg, _, mine, other, sem):
    c = lax.axis_index("dp") % 2
    rows, length = w.shape[0], seg.shape[1]
    other[rows:, :length] = jnp.broadcast_to(seg[...].astype(f32), (ID_ROWS, length)).astype(bf16)
    copies = []
    for target, which in ((mine, c), (other, 1 - c)):
        copies += [(w.at[:, kv_columns(n, which)], target.at[:rows, head(n)]) for n in range(4)]
    copies += [(w.at[:, columns(2 * g + 1 - c, HEAD_DIM)], other.at[:rows, head(4 + g)]) for g in range(2)]
    run_all(copies, sem)


def split_q_body(w, mine, other, sem):
    c = lax.axis_index("dp") % 2
    copies = []
    for target, which in ((mine, c), (other, 1 - c)):
        copies += [(w.at[:, columns(2 * g + which, HEAD_DIM)], target.at[:, head(g)]) for g in range(2)]
    run_all(copies, sem)


def split(body, shapes, copies, us, w, *rest, specs=()):
    return pl.pallas_call(
        body,
        out_shape=[jax.ShapeDtypeStruct(shape, bf16) for shape in shapes],
        in_specs=[ANY, *specs],
        out_specs=[VMEM] * len(shapes),
        scratch_shapes=[pltpu.SemaphoreType.DMA((copies,))],
        compiler_params=pltpu.CompilerParams(vmem_limit_bytes=8 * 1024 * 1024),
        cost_estimate=pl.CostEstimate(flops=int(us * 1e9), transcendentals=0, bytes_accessed=10**6),
    )(w, *rest)


KV_COLUMNS = slice(0, 4 * HEAD_DIM)
PAIR_Q = slice(4 * HEAD_DIM, 6 * HEAD_DIM)


def halves():
    at = lax.axis_index("groups")
    return at, 1 - at


def sources(step):
    at, n = lax.axis_index("seq"), lax.axis_size("seq")
    if n != 4:
        return at < 0, at < 0
    return (at % 2 == 1, at >= 2) if step > 0 else (at % 2 == 0, at < 2)


def pair_body(near, normed, seg, w1, raw, seg_col, seg_row):
    rows, length = w1.shape[0] - ID_ROWS, seg.shape[1]
    for i, ids in enumerate((seg[...].astype(f32), w1[rows : rows + 1, :length].astype(f32))):
        seg_row[i] = ids
        seg_col[i] = jnp.broadcast_to(ids, (HEAD_DIM, length)).T
    raw[...] = near[...] + dot_nn(normed[1], w1[:rows, KV_COLUMNS])


def prep_body(tokens, partner, gain, w0, normed, inv_rms, raw):
    length = tokens.shape[0]
    for i, part in enumerate((tokens, partner)):
        x = part[...].astype(f32)
        inv = lax.rsqrt(jnp.mean(x * x, axis=1, keepdims=True) + epsilon)
        if i == 0:
            inv_rms[...] = inv
        for j in range(4):
            at = columns(lax.axis_index("dp") ^ j, 256)
            normed[j, i * length : (i + 1) * length] = (part[:, at].astype(f32) * inv * gain[:, at]).astype(bf16)
    raw[...] = dot_nn(normed[0], w0[...])


def store_state(targets, i, g, value):
    for target in targets:
        target[i, head(g), :] = value.astype(bf16)


def store_ids(targets, i, ids):
    for target in targets:
        rows = target.shape[1] - 2 * HEAD_DIM
        target[i, 2 * HEAD_DIM :, :] = jnp.broadcast_to(ids, (rows, HEAD_DIM)).astype(bf16)


def kv_body(near, normed, w2, w3, w3_other, seg_col, feat_k, values, state, state_mid, state_far):
    length = seg_col.shape[1]
    raw = near[...] + dot_nn(normed[2], w2[...])
    for at, w in zip(halves(), (w3, w3_other)):
        raw += dot_nn(normed[3, :, columns(at, w.shape[0])], w[...])
    raw = raw.astype(bf16)
    for i in range(2):
        last = seg_col[i, length - 1 : length, :]
        tail = seg_col[i] == last
        rows = slice(i * length, (i + 1) * length)
        for g in range(2):
            k = feature_map(raw[rows, head(g)].astype(f32))
            v = raw[rows, head(2 + g)]
            feat_k[i, g] = k.astype(bf16)
            values[i, g] = v
            store_state((state, state_mid, state_far), i, g, dot_tn(jnp.where(tail, k, 0.0).astype(bf16), v))
        store_ids((state, state_mid, state_far), i, last)


def query_body(normed, w0, w1, w2, w3, feat_k, values, seg_col, seg_row, feat_q, intra):
    raw = dot_nn(normed[0], w0[...]) + dot_nn(normed[1], w1[: w0.shape[0], PAIR_Q])
    raw += dot_nn(normed[2], w2[...]) + dot_nn(normed[3], w3[...])
    raw = raw.astype(bf16)
    length = seg_row.shape[2]
    for i in range(2):
        mask = causal(seg_col, seg_row, i)
        for g in range(2):
            q = feature_map(raw[i * length : (i + 1) * length, head(g)].astype(f32)).astype(bf16)
            feat_q[i, g] = q
            s = jnp.where(mask, dot_nt(q, feat_k[i, g]), 0.0).astype(bf16)
            intra[i, g] = dot_nn(s, values[i, g])


def mixed_grad_body(cot, cot_partner, own, other, gain, upstream):
    for j, o in enumerate((own, other)):
        full = lax.axis_index("dp") ^ (2 * j)
        for i, part in enumerate((cot, cot_partner)):
            upstream[i, full // 2] = dot_nt(part[...], o[...]) * gain[:, columns(full, HEAD_DIM)]


def received(step, pair, middle, further, i):
    use_pair, use_further = sources(step)
    used = 2 * HEAD_DIM + ID_ROWS
    near = jnp.where(use_pair, pair[i, :used].astype(f32), middle[i, :used].astype(f32))
    ids = near[2 * HEAD_DIM : 2 * HEAD_DIM + 1, :]
    far = further[i, :used].astype(f32)
    same = (far[2 * HEAD_DIM : 2 * HEAD_DIM + 1, :] == ids) & use_further
    total = near[: 2 * HEAD_DIM] + jnp.where(same, far[: 2 * HEAD_DIM], 0.0)
    return ids, total.astype(bf16)


def attn_body(
    pair, middle, further, seg_col, feat_q, intra, upstream, gain, cot, cot_partner,
    mixed, d_attn, state, state_mid, state_far, before, rest, a_send, b_send,
):
    for i in range(2):
        first = seg_col[i, 0:1, :]
        begin = seg_col[i] == first
        ids, total = received(1, pair, middle, further, i)
        before[i] = total
        take = seg_col[i] == ids
        for g in range(2):
            q = feat_q[i, g]
            attention = intra[i, g] + jnp.where(take, dot_nn(q, total[head(g)]), 0.0)
            ratio = lax.rsqrt(jnp.mean(attention * attention, axis=1, keepdims=True) + epsilon)
            mixed[i, g] = (attention * ratio * gain[:, columns(2 * g + lax.axis_index("dp") % 2, HEAD_DIM)]).astype(bf16)
            up = upstream[i, g]
            inner = jnp.mean(attention * up, axis=1, keepdims=True)
            da = (ratio * up - ratio**3 * attention * inner).astype(bf16)
            d_attn[i, g] = da
            store_state((state, state_mid, state_far), i, g, dot_tn(jnp.where(begin, q.astype(f32), 0.0).astype(bf16), da))
        store_ids((state, state_mid, state_far), i, first)
    half = HEAD_DIM // 2
    quarter = half // 2
    second = lax.axis_index("seq") % 2 == 1
    for j in range(2):
        g = (lax.axis_index("dp") ^ (2 * j)) // 2
        part = dot_tn(mixed[0, g], cot[...]) + dot_tn(mixed[1, g], cot_partner[...])
        if j == 0:
            rest[:half] = part[:half]
        else:
            a_send[...] = part[:half].astype(bf16)
        low, high = part[half : half + quarter], part[half + quarter :]
        rest[half + j * quarter : half + (j + 1) * quarter] = jnp.where(second, high, low)
        b_send[j] = jnp.where(second, low, high).astype(bf16)


def weight_one_body(rest, a_in, b_in, kept, a_send, b_send):
    second = lax.axis_index("seq") % 2 == 1
    quarter = b_in.shape[1]
    low = rest[:quarter] + a_in[:quarter].astype(f32)
    high = rest[quarter : 2 * quarter] + a_in[quarter:].astype(f32)
    kept[:quarter] = jnp.where(second, high, low)
    a_send[...] = jnp.where(second, low, high).astype(bf16)
    kept[quarter:] = rest[2 * quarter : 3 * quarter] + b_in[0].astype(f32)
    b_send[...] = (rest[3 * quarter :] + b_in[1].astype(f32)).astype(bf16)


def weight_two_body(kept, a_in, b_in, total, send):
    quarter = a_in.shape[0]
    total[:quarter] = kept[:quarter] + a_in[...].astype(f32)
    total[quarter:] = kept[quarter:] + b_in[...].astype(f32)
    send[...] = total[...].astype(bf16)


def weight_three_body(kept, arrived, total, send):
    total[...] = kept[...] + arrived[...].astype(f32)
    send[...] = total[...].astype(bf16)


def weight_last_body(scale, kept, arrived, grad):
    quarter = kept.shape[0] // 2
    second = lax.axis_index("seq") % 2 == 1
    mine, theirs = kept[...] * scale, arrived[...].astype(f32) * scale
    low = jnp.where(second, theirs, mine)
    high = jnp.where(second, mine, theirs)
    for n, part in enumerate((low[:quarter], high[:quarter], low[quarter:], high[quarter:])):
        grad[n * quarter : (n + 1) * quarter] = part


def back_body(
    pair, before, middle, seg_col, seg_row, d_attn, values, feat_k, feat_q,
    d_query, dk_intra, dv_intra,
):
    for i in range(2):
        mask = causal(seg_col, seg_row, i)
        use_pair, _ = sources(1)
        last = 2 * HEAD_DIM
        ids = jnp.where(use_pair, pair[i, last : last + 1].astype(f32), middle[i, last : last + 1].astype(f32))
        take = seg_col[i] == ids
        for g in range(2):
            da, q, k = d_attn[i, g], feat_q[i, g], feat_k[i, g]
            s = jnp.where(mask, dot_nt(q, k), 0.0).astype(bf16)
            ds = jnp.where(mask, dot_nt(da, values[i, g]), 0.0).astype(bf16)
            dq = dot_nn(ds, k) + jnp.where(take, dot_nt(da, before[i, head(g)]), 0.0)
            d_query[i, :, head(g)] = (dq * jnp.minimum(q.astype(f32), 1.0)).astype(bf16)
            dk_intra[i, g] = dot_tn(ds, q)
            dv_intra[i, g] = dot_tn(s, da)


def partner_output_body(mixed, own, other, out_partner):
    x = lax.axis_index("dp") // 2
    out_partner[...] = (dot_nn(mixed[1, x], own[...]) + dot_nn(mixed[1, 1 - x], other[...])).astype(bf16)


def project_back_body(
    pair, middle, further, seg_col, feat_k, values, dk_intra, dv_intra, d_query,
    q0, q1, q2, q3, w0, w1, w2, w3, w3_other, own, partner, work,
):
    q = (q0[...], q1[: w0.shape[0], PAIR_Q], q2[...], q3[...])
    w = (w0[...], w1[: w0.shape[0], KV_COLUMNS], w2[...])
    for i in (1, 0):
        ids, total = received(-1, pair, middle, further, i)
        take = seg_col[i] == ids
        d_key, d_value = [], []
        for g in range(2):
            back = total[head(g)]
            k, v = feat_k[i, g], values[i, g]
            dk = dk_intra[i, g] + jnp.where(take, dot_nt(v, back), 0.0)
            dv = dv_intra[i, g] + jnp.where(take, dot_nn(k, back), 0.0)
            d_key.append((dk * jnp.minimum(k.astype(f32), 1.0)).astype(bf16))
            d_value.append(dv.astype(bf16))
        d_proj = jnp.concatenate(d_key + d_value, axis=1)
        pieces = [(j, slice(None), dot_nt(d_proj, w[j])) for j in range(3)]
        pieces += [
            (3, columns(at, part.shape[0]), dot_nt(d_proj, part[...])) for at, part in zip(halves(), (w3, w3_other))
        ]
        for j in range(4):
            from_q = dot_nt(d_query[i], q[j])
            if i == 1:
                work[j ^ 1] = from_q
            else:
                own[j] = from_q
        for j, at, value in pieces:
            if i == 1:
                partner[j ^ 1, :, at] = (work[j ^ 1, :, at] + value).astype(bf16)
            else:
                own[j, :, at] += value


def final_body(
    own, partner, out_partner, tokens, cot, inv_rms, gain, mixed, w_own, w_other, output, grad, work
):
    x = lax.axis_index("dp") // 2
    total = dot_nn(mixed[0, x], w_own[...]) + dot_nn(mixed[0, 1 - x], w_other[...])
    output[...] = (tokens[...].astype(f32) + (total + out_partner[...].astype(f32))).astype(bf16)
    inner = None
    for j in range(4):
        at = columns(lax.axis_index("dp") ^ j, 256)
        norm_grad = (own[j] + partner[j].astype(f32)) * gain[:, at]
        work[j] = norm_grad
        part = jnp.sum(tokens[:, at].astype(f32) * norm_grad, axis=1, keepdims=True)
        inner = part if inner is None else inner + part
    inv = inv_rms[...]
    scale = inv**3 * (inner * (1.0 / D))
    for j in range(4):
        at = columns(lax.axis_index("dp") ^ j, 256)
        value = cot[:, at].astype(f32) + inv * work[j] - tokens[:, at].astype(f32) * scale
        grad[:, at] = value.astype(bf16)


def flip(array, axis, bit):
    n = lax.axis_size(axis)
    return lax.ppermute(array, axis, [(i, i ^ bit) for i in range(n)])


def shift(array, axis, step):
    n = lax.axis_size(axis)
    return lax.ppermute(array, axis, [(i, i + step) for i in range(n) if 0 <= i + step < n])


def carry(message, middle, further, ends, step, late=None):
    n = lax.axis_size("seq")
    if n == 4:
        middle = lax.ppermute(middle, "seq", [(1, 2), (2, 1)])
        return flip(message if late is None else late, "seq", 1), middle, flip(further, "seq", 2)
    position = lax.axis_index("seq")
    begin, end = (ends[0], ends[1]) if step > 0 else (ends[1], ends[0])
    total = message[:, : 2 * HEAD_DIM].astype(f32)
    reach = 1
    while reach < n:
        before = shift(total, "seq", step * reach)
        ids = shift(jnp.stack([begin, end]), "seq", step * reach)
        there = position - step * reach
        there = (there >= 0) & (there < n)
        goes_on = there & (begin == end) & (ids[1] == begin)
        total = total + jnp.where(goes_on[:, None, None], before, 0.0)
        begin = jnp.where(there, ids[0], begin)
        reach *= 2
    rows = jnp.concatenate([total.astype(bf16), message[:, 2 * HEAD_DIM :]], axis=1)
    near = shift(rows, "seq", step)
    return near, near, near


def reduce_weight(rest, a_send, b_send, back, ends, d_attn):
    n = lax.axis_size("seq")
    half, width = a_send.shape
    quarter = half // 2
    kept, a_send, b_send = call(
        weight_one_body,
        [((half, width), f32), ((quarter, width), bf16), ((quarter, width), bf16)],
        rest, flip(a_send, "dp", 2), flip(b_send, "seq", 1), us=W1,
    )
    a_send, back_late = lax.optimization_barrier((a_send, back[0]))
    back_near = carry(*back, ends, -1, back_late)
    outs = [((half, width), f32), ((half, width), bf16)]
    kept, send = call(weight_two_body, outs, kept, flip(a_send, "seq", 1), flip(b_send, "dp", 2), us=W2)
    send, d_attn = lax.optimization_barrier((send, d_attn))
    reach = 2
    while reach < n:
        kept, send = call(weight_three_body, outs, kept, flip(send, "seq", reach), us=W3)
        reach *= 2
    return kept, send, back_near, d_attn


def shards(tokens, segment_ids, norm_gain, w_qkv, head_gain, w_out, cotangent):
    length = segment_ids.shape[1]
    width = HEADS * HEAD_DIM
    n = lax.axis_size("seq")
    flat = tokens.reshape(length, D)
    cot = cotangent.reshape(length, D)
    gain = norm_gain.reshape(1, D)
    gain_h = head_gain.reshape(1, width)
    wide = (2, 2, length, HEAD_DIM)

    shard_rows = w_qkv.shape[0]
    w_first = pltpu.with_memory_space_constraint(w_qkv, pltpu.HBM)
    (kv_half,) = split(split_half_body, [(shard_rows // 2, 4 * HEAD_DIM)], 4, 1.0, w_first)
    kv_diagonal = flip(kv_half, "dp", 3)
    kv_mine, kv_other = split(
        split_kv_body,
        [(shard_rows, 4 * HEAD_DIM), (shard_rows + ID_ROWS, 6 * HEAD_DIM)],
        10, SPLIT, w_qkv, segment_ids, kv_half, specs=(VMEM, ANY),
    )
    kv_half, flat, cot = lax.optimization_barrier((kv_half, flat, cot))
    kv_x, kv_pair = flip(kv_mine, "dp", 2), flip(kv_other, "dp", 1)
    partner, cot_partner = flip(flat, "dp", 1), flip(cot, "dp", 1)
    partner, cot_partner, w_late = lax.optimization_barrier((partner, cot_partner, w_qkv))
    normed, inv_rms, raw_near = call(
        prep_body,
        [((4, 2 * length, D // 4), bf16), ((length, 1), f32), ((2 * length, 4 * HEAD_DIM), f32)],
        flat, partner, gain, kv_mine, us=PREP,
    )
    kv_diagonal, inv_rms = lax.optimization_barrier((kv_diagonal, inv_rms))
    kv_diagonal_other = flip(kv_diagonal, "groups", 1)
    raw_near, seg_col, seg_row = call(
        pair_body,
        [((2 * length, 4 * HEAD_DIM), f32), ((2, length, HEAD_DIM), f32), ((2, 1, length), f32)],
        raw_near, normed, segment_ids, kv_pair,
    )
    q_mine, q_other = split(split_q_body, [(shard_rows, 2 * HEAD_DIM)] * 2, 4, 1.0, w_late)
    raw_near, q_mine, q_other, out_own = lax.optimization_barrier((raw_near, q_mine, q_other, w_out))
    wq = [q_mine, kv_pair, flip(q_mine, "dp", 2), flip(q_other, "dp", 3)]
    kv = [kv_mine, kv_pair, kv_x, kv_diagonal, kv_diagonal_other]
    out = [out_own, flip(out_own, "dp", 2)]

    messages = [((2, 2 * HEAD_DIM + m * ID_ROWS, HEAD_DIM), bf16) for m in (1, 1, 2)]
    feat_k, values, state, state_mid, state_far = call(
        kv_body, [(wide, bf16), (wide, bf16), *messages], raw_near, normed, *kv[2:], seg_col
    )
    ends = jnp.stack([seg_col[:, 0, 0], seg_col[:, -1, 0]])
    near = carry(state, state_mid, state_far, ends, 1)
    feat_q, intra = call(
        query_body, [(wide, bf16), (wide, f32)], normed, *wq, feat_k, values, seg_col, seg_row, us=QUERY
    )
    feat_q, cot_late = lax.optimization_barrier((feat_q, cot_partner))
    (upstream,) = call(
        mixed_grad_body, [(wide, f32)], cot, cot_late, *out, gain_h, us=MIXED
    )
    rows = HEAD_DIM // 2
    mixed, d_attn, back, back_mid, back_far, before, rest, a_send, b_send = call(
        attn_body,
        [
            (wide, bf16),
            (wide, bf16),
            *messages,
            ((2, 2 * HEAD_DIM, HEAD_DIM), bf16),
            ((2 * rows, D), f32),
            ((rows, D), bf16),
            ((2, rows // 2, D), bf16),
        ],
        *near, seg_col, feat_q, intra, upstream, gain_h, cot, cot_partner,
    )
    scale = 1.0 / math.sqrt(length * lax.axis_size("dp") * n)
    kept, sent, back_near, d_attn = reduce_weight(rest, a_send, b_send, (back, back_mid, back_far), ends, d_attn)
    (out_partner,) = call(partner_output_body, [((length, D), bf16)], mixed, *out, us=FILL)
    d_query, dk_intra, dv_intra = call(
        back_body,
        [((2, length, 2 * HEAD_DIM), bf16), (wide, f32), (wide, f32)],
        near[0], before, near[1], seg_col, seg_row, d_attn, values, feat_k, feat_q, us=BACK,
    )
    own, theirs = call(
        project_back_body,
        [((4, length, D // 4), f32), ((4, length, D // 4), bf16)],
        *back_near, seg_col, feat_k, values, dk_intra, dv_intra, d_query,
        *wq, *kv, us=PROJECT, scratch=[((4, length, D // 4), f32)],
    )
    theirs, out_partner = lax.optimization_barrier((theirs, out_partner))
    output, grad = call(
        final_body,
        [((length, D), bf16), ((length, D), bf16)],
        own, flip(theirs, "dp", 1), flip(out_partner, "dp", 1), flat, cot, inv_rms, gain, mixed, *out,
        scratch=[((4, length, D // 4), f32)],
    )
    arrived = flip(sent, "seq", 1)
    output, grad, kept = lax.optimization_barrier((output, grad, kept))
    (grad_out_weight,) = call(
        functools.partial(weight_last_body, scale), [((HEAD_DIM, D), f32)], kept, arrived
    )
    return (output.reshape(tokens.shape), grad.reshape(tokens.shape), grad_out_weight)


def solution(mesh):
    in_specs = (
        P(("groups", "dp"), "seq", None),
        P(("groups", "dp"), "seq"),
        P(),
        P("dp", None),
        P(),
        P("dp", None),
        P(("groups", "dp"), "seq", None),
    )
    out_specs = (
        P(("groups", "dp"), "seq", None),
        P(("groups", "dp"), "seq", None),
        P(("groups", "dp"), None),
    )
    return jax.shard_map(shards, mesh=mesh, in_specs=in_specs, out_specs=out_specs, check_vma=False)
```
